256 devices in a mesh: batch: 8 (over y, z_lo), seq: 32 (over z_hi, x, core).
Axes of the slice: x: 4, y: 4, z: 8 (z_hi: 4, z_lo: 2; z = z_hi * 2 + z_lo), core: 2. Of those that a mesh axis runs over, the one named last changes fastest.
Arguments:
- tokens: bfloat16 [2048, 256, 768], P(('batch', 'seq')), parts along dimension 0, may hold values from -6 to 6
- cotangent: bfloat16 [2048, 256, 768], P(('batch', 'seq')), parts along dimension 0, may hold values from -6 to 6
- gate_taps: float32 [3, 768], replicated, may hold values from -3.5 to 3.5
- key_taps: float32 [3, 768], replicated, may hold values from -3.5 to 3.5
- value_taps: float32 [3, 768], replicated, may hold values from -3.5 to 3.5
- inner_mix: bfloat16 [256, 256], replicated, may hold values from -0.375 to 0.375
- outer_mix: bfloat16 [256, 256], replicated, may hold values from -0.375 to 0.375
- spectrum: float32 [256, 768], replicated, may hold values from 0.5 to 2
Outputs:
- grad_tokens: bfloat16 [2048, 256, 768], P(('batch', 'seq')), parts along dimension 0
- grad_gate_taps: float32 [24, 768], P('batch'), parts along dimension 0
- grad_key_taps: float32 [24, 768], P('batch'), parts along dimension 0
- grad_value_taps: float32 [24, 768], P('batch'), parts along dimension 0
- grad_inner_mix: float32 [2048, 256], P('batch'), parts along dimension 0
- grad_outer_mix: float32 [2048, 256], P('batch'), parts along dimension 0
- grad_spectrum: float32 [2048, 768], P('batch'), parts along dimension 0
The draws below stay inside these ranges and needn't reach their ends.
There are 8 independent parts, one for each index of `batch`. The reference program is written for one: setup_inputs(seed, part) draws one part's arguments, and reference() takes and returns one part's arrays. A program takes and returns all parts, laid end to end along the dimension named above; an argument that names none is the same for every part. Nothing has to cross between parts.
All inputs are finite; a program needn't handle non-finite values.
Results may differ from the reference program's by a relative error of at most 0.0064.
Values may be sent and summed in bfloat16 or wider, within the bound.
A program may use at most 128 MiB of HBM per device.

```python
import math
import jax
import jax.numpy as jnp
from jax import lax

B = 256
NB = 256
C = 768


def block_scale(key, shape, cuts, least, largest):
    level = 1.0
    for dim, blocks in cuts:
        heights = jax.random.uniform(jax.random.fold_in(jax.random.fold_in(key, 6), dim), (blocks,), jnp.float32, least / len(cuts), largest / len(cuts))
        level = level * jnp.repeat(jnp.exp(heights), shape[dim] // blocks).reshape((-1,) + (1,) * (len(shape) - 1 - dim))
    return level


def gaussian(rng, shape, scale, reach, cuts=(), held_as=jnp.bfloat16):
    drawn = jax.random.normal(rng, shape, jnp.float32) * scale
    if len(cuts) > 0:
        drawn = block_scale(rng, shape, cuts, -0.22, 0.18) * drawn
    return jnp.clip(drawn, min=-reach, max=reach).astype(held_as)


def setup_inputs(seed: int = 0, part: int = 0) -> dict:
    seeds = jax.random.split(jax.random.key(seed), 9)
    own_keys = jax.random.split(jax.random.fold_in(seeds[8], part), 9)
    tokens = gaussian(own_keys[0], (NB, B, C), 1.0, 6.0, ((0, 32),))
    cotangent = gaussian(own_keys[1], (NB, B, C), 1.0, 6.0, ((0, 32),))
    gate_taps = gaussian(seeds[2], (3, C), 3 ** -0.5, 3.5, (), jnp.float32)
    key_taps = gaussian(seeds[3], (3, C), 3 ** -0.5, 3.5, (), jnp.float32)
    value_taps = gaussian(seeds[4], (3, C), 3 ** -0.5, 3.5, (), jnp.float32)
    inner_mix = gaussian(seeds[5], (B, B), B ** -0.5, 0.375)
    outer_mix = gaussian(seeds[6], (NB, NB), NB ** -0.5, 0.375)
    spectrum = jnp.clip(jnp.exp(jax.random.uniform(seeds[7], (B, C), jnp.float32, math.log(0.5), math.log(2.0))), 0.5, 2.0)
    return dict(tokens=tokens, cotangent=cotangent, gate_taps=gate_taps, key_taps=key_taps, value_taps=value_taps, inner_mix=inner_mix, outer_mix=outer_mix, spectrum=spectrum)


def causal_matrix(weights):
    extent = weights.shape[0]
    lower_part = jnp.tril(jnp.ones((extent, extent), jnp.bool_), -1)
    return jnp.where(lower_part, weights.astype(jnp.float32), jnp.eye(extent, dtype=jnp.float32))

def strict_lower(extent):
    return jnp.tril(jnp.ones((extent, extent), jnp.float32), -1)

def conv_forward(padded, taps):
    return taps[0] * padded[2:] + taps[1] * padded[1:-1] + taps[2] * padded[:-2]

def conv_backward(padded_grad, taps):
    return taps[0] * padded_grad[:-2] + taps[1] * padded_grad[1:-1] + taps[2] * padded_grad[2:]

def taps_grad(grad_rows, padded):
    count = grad_rows.shape[0]
    return jnp.stack([lax.optimization_barrier(jnp.sum(grad_rows * padded[2 - shift_by:2 - shift_by + count], axis=0)) for shift_by in range(3)])

def reference(tokens, cotangent, gate_taps, key_taps, value_taps, inner_mix, outer_mix, spectrum):
    channels = tokens.shape[2]
    token_rows = tokens.reshape(NB * B, channels).astype(jnp.float32)
    padded = jnp.concatenate([jnp.zeros((2, channels), jnp.float32), token_rows], 0)
    gate_conv = conv_forward(padded, gate_taps)
    key_conv = conv_forward(padded, key_taps)
    value_conv = conv_forward(padded, value_taps)
    product = (key_conv * value_conv).astype(jnp.bfloat16).reshape(NB, B, channels).astype(jnp.float32)
    first_mix = causal_matrix(inner_mix)
    second_mix = causal_matrix(outer_mix)
    pre_scale = jnp.einsum('jk,ikc->ijc', first_mix, product)
    inner_out = (pre_scale * spectrum).astype(jnp.bfloat16).astype(jnp.float32)
    mixed_out = jnp.einsum('ik,kjc->ijc', second_mix, inner_out).astype(jnp.bfloat16).astype(jnp.float32)
    cot_values = cotangent.astype(jnp.float32)
    gate_block = gate_conv.reshape(NB, B, channels)
    grad_mixed = (cot_values * gate_block).astype(jnp.bfloat16).astype(jnp.float32)
    grad_inner = jnp.einsum('ki,kjc->ijc', second_mix, grad_mixed).astype(jnp.bfloat16).astype(jnp.float32)
    grad_outer_mix = jnp.einsum('ijc,kjc->ik', grad_mixed, inner_out) * strict_lower(NB)
    grad_spectrum = lax.optimization_barrier(jnp.sum(grad_inner * pre_scale, axis=0))
    grad_scaled = (grad_inner * spectrum).astype(jnp.bfloat16).astype(jnp.float32)
    grad_inner_mix = jnp.einsum('ijc,ikc->jk', grad_scaled, product) * strict_lower(B)
    grad_product = jnp.einsum('jk,ijc->ikc', first_mix, grad_scaled).reshape(NB * B, channels)
    grad_gate = (cot_values * mixed_out).reshape(NB * B, channels)
    grad_key = grad_product * value_conv
    grad_value = grad_product * key_conv
    tail = jnp.zeros((2, channels), jnp.float32)
    grad_rows = conv_backward(jnp.concatenate([grad_gate, tail], 0), gate_taps)
    grad_rows = grad_rows + conv_backward(jnp.concatenate([grad_key, tail], 0), key_taps)
    grad_rows = grad_rows + conv_backward(jnp.concatenate([grad_value, tail], 0), value_taps)
    grad_tokens = grad_rows.reshape(NB, B, channels).astype(jnp.bfloat16)
    return (grad_tokens, taps_grad(grad_gate, padded), taps_grad(grad_key, padded), taps_grad(grad_value, padded), grad_inner_mix, grad_outer_mix, grad_spectrum)
```

```python
import jax
import jax.numpy as jnp
from jax import lax
from jax.experimental import pallas as pl
from jax.experimental.pallas import tpu as pltpu
from jax.sharding import PartitionSpec as P

MESH = pl.DeviceIdType.MESH
F32 = jnp.float32
BF16 = jnp.bfloat16

LEN = 256
CHIPS = 16
LANES = 128
CHUNKS = 3
HALF = LANES * CHUNKS
ROWS = CHIPS * LEN
OWN = ROWS // 2
HALO = 16


def dot(a, b):
    return jnp.dot(a, b, preferred_element_type=F32)


def dot_lanes(a, b):
    return lax.dot_general(a, b, (((1,), (1,)), ((), ())), preferred_element_type=F32)


def strict_lower(value, first_row):
    rows = lax.broadcasted_iota(jnp.int32, value.shape, 0) + first_row
    cols = lax.broadcasted_iota(jnp.int32, value.shape, 1)
    return jnp.where(rows > cols, value, 0.0)


def kernel(
    tok, cot, gate_taps, key_taps, value_taps, inner_mix, outer_mix, spectrum,
    out_tok, out_gate, out_key, out_value, out_inner, out_outer, out_spec,
    T, CT, PR, AB, S, Z, R, F, GT, MAT, CARRY, HB, HR, LB, TA,
    inner_acc, outer_acc, SG, sib_sum, red_send, red_recv, red_sum, gathered, gathered_sib,
    sg_all, sg_sib,
    in_sem, in_send, halo_sem, halo_send, z_sem, s_send, f_sem, r_send, hb_sem, hb_send,
    out_local, out_send, out_recv, sib_sem, sib_send, rs_sem, rs_send, ag_sem, ag_send,
    gx_sem, gx_send, sg_sem, sg_send, sgx_sem, sgx_send,
):
    batch = lax.axis_index("batch")
    seq = lax.axis_index("seq")
    core = seq % 2
    chip = seq // 2
    cz = chip // 4
    cx = chip % 4
    other = 1 - core
    sibling = (batch, chip * 2 + other)

    def chip_dev(q):
        return (batch, q * 2 + core)

    def peer(d):
        return ((cz + d // 4) % 4) * 4 + (cx + d % 4) % 4

    barrier = pltpu.get_barrier_semaphore()

    def greet(d, carry):
        pl.semaphore_signal(barrier, inc=1, device_id=chip_dev(peer(d)), device_id_type=MESH)
        return carry

    lax.fori_loop(1, CHIPS, greet, 0)
    pl.semaphore_signal(barrier, inc=1, device_id=sibling, device_id_type=MESH)
    pl.semaphore_wait(barrier, CHIPS)

    def remote(src, dst, send, recv, device):
        return pltpu.make_async_remote_copy(
            src_ref=src, dst_ref=dst, send_sem=send, recv_sem=recv,
            device_id=device, device_id_type=MESH,
        )

    def wait_bytes(ref, sem):
        pltpu.make_async_copy(ref, ref, sem).wait()

    my_rows = pl.ds(pl.multiple_of(core * OWN, OWN), OWN)
    halo_rows = pl.ds(pl.multiple_of(HALO + core * OWN, HALO), OWN)

    def lanes_of(c, ch):
        return pl.ds(pl.multiple_of(c * HALF + ch * LANES, LANES), LANES)

    def start_inputs(ch, carry):
        remote(tok.at[:, lanes_of(other, ch)], T.at[ch, halo_rows], in_send.at[ch, 0], in_sem.at[ch, 0], sibling).start()
        remote(cot.at[:, lanes_of(other, ch)], CT.at[ch, my_rows], in_send.at[ch, 1], in_sem.at[ch, 1], sibling).start()
        pltpu.make_async_copy(tok.at[:, lanes_of(core, ch)], T.at[ch, halo_rows], in_sem.at[ch, 0]).start()
        pltpu.make_async_copy(cot.at[:, lanes_of(core, ch)], CT.at[ch, my_rows], in_sem.at[ch, 1]).start()
        return carry

    lax.fori_loop(0, CHUNKS, start_inputs, 0)

    row_id = lax.broadcasted_iota(jnp.int32, (LEN, LEN), 0)
    col_id = lax.broadcasted_iota(jnp.int32, (LEN, LEN), 1)
    for at, weights in ((0, inner_mix), (2, outer_mix)):
        full = jnp.where(
            row_id > col_id, weights[...].astype(F32), jnp.where(row_id == col_id, 1.0, 0.0)
        )
        MAT[at] = full.astype(BF16)
        MAT[at + 1] = jnp.transpose(full).astype(BF16)
    MAT[4] = jnp.where(col_id == (row_id % 16) * 16 + row_id // 16, 1.0, 0.0).astype(BF16)
    inner_acc[...] = jnp.zeros_like(inner_acc)
    outer_acc[...] = jnp.zeros_like(outer_acc)
    TA[...] = jnp.zeros_like(TA)

    def send_halo(ch, carry):
        wait_bytes(T.at[ch, pl.ds(HALO, ROWS)], in_sem.at[ch, 0])

        @pl.when(chip < CHIPS - 1)
        def _():
            remote(
                T.at[ch, pl.ds(ROWS, HALO)], T.at[ch, pl.ds(0, HALO)],
                halo_send.at[ch], halo_sem.at[ch], chip_dev(chip + 1),
            ).start()

        @pl.when(chip == 0)
        def _():
            T[ch, 0:HALO] = jnp.zeros((HALO, LANES), BF16)

        wait_bytes(CT.at[ch], in_sem.at[ch, 1])
        return carry

    def taps_of(ref, ch):
        block = ref[:, lanes_of(core, ch)]
        return block[0:1], block[1:2], block[2:3]

    def shifted_rows(ch, i):
        ext = T[ch, pl.ds(pl.multiple_of(i * LEN, LEN), LEN + HALO)].astype(F32)
        return ext[HALO:], pltpu.roll(ext, 1, 0)[HALO:], pltpu.roll(ext, 2, 0)[HALO:]

    def conv(taps, x):
        return taps[0] * x[0] + taps[1] * x[1] + taps[2] * x[2]

    def block_rows(i):
        return pl.ds(pl.multiple_of(i * LEN, LEN), LEN)

    def before(ch, carry):
        gt, kt, vt = taps_of(gate_taps, ch), taps_of(key_taps, ch), taps_of(value_taps, ch)
        send_halo(ch, 0)

        def pair(step, c):
            p = CHIPS // 2 - 1 - step

            @pl.when(jnp.logical_and(p == 0, chip > 0))
            def _():
                wait_bytes(T.at[ch, pl.ds(0, HALO)], halo_sem.at[ch])

            products = []
            for b in range(2):
                i = 2 * p + b
                x = shifted_rows(ch, i)
                product = (conv(kt, x) * conv(vt, x)).astype(BF16)
                PR[ch, block_rows(i)] = product
                products.append(product)
                grad_mixed = CT[ch, block_rows(i)].astype(F32) * conv(gt, x)
                AB[i, :, LANES:] = grad_mixed.astype(BF16)
            pre = dot(MAT[0], jnp.concatenate(products, 1))
            scale = spectrum[:, lanes_of(core, ch)]
            for b in range(2):
                AB[2 * p + b, :, :LANES] = (pre[:, b * LANES:(b + 1) * LANES] * scale).astype(BF16)
            return c

        lax.fori_loop(0, CHIPS // 2, pair, 0)

        def regroup(j, c):
            rows = AB[:, pl.ds(pl.multiple_of(j * 16, 16), 16)].reshape(LEN, 2 * LANES)
            S[ch, j] = dot(MAT[4], rows).astype(BF16).reshape(16, 16, 2 * LANES)
            return c

        lax.fori_loop(0, CHIPS, regroup, 0)
        mine = pl.ds(pl.multiple_of(chip * 16, 16), 16)

        def send(d, c):
            q = peer(d)
            remote(S.at[ch, q], Z.at[ch, :, mine], s_send.at[ch], z_sem.at[ch], chip_dev(q)).start()
            return c

        lax.fori_loop(1, CHIPS, send, 0)
        pltpu.make_async_copy(S.at[ch, chip], Z.at[ch, :, mine], z_sem.at[ch]).start()
        return carry

    lax.fori_loop(0, CHUNKS, before, 0)

    def across(ch, carry):
        wait_bytes(Z.at[ch], z_sem.at[ch])
        scale = spectrum[pl.ds(pl.multiple_of(chip * 16, 16), 16), lanes_of(core, ch)]

        def pair(p, c):
            j = 2 * p
            z0, z1 = Z[ch, j], Z[ch, j + 1]
            inner = jnp.concatenate([z0[:, :LANES], z1[:, :LANES]], 1)
            grads = jnp.concatenate([z0[:, LANES:], z1[:, LANES:]], 1)
            mixed = dot(MAT[2], inner).astype(BF16)
            grad_inner = dot(MAT[3], grads).astype(BF16)
            outer_acc[...] += dot_lanes(grads, inner)
            terms = jnp.sum(grad_inner.astype(F32) * inner.astype(F32), axis=0, keepdims=True)
            for b in range(2):
                at = slice(b * LANES, (b + 1) * LANES)
                R[ch, j + b, :, :LANES] = mixed[:, at]
                R[ch, j + b, :, LANES:] = grad_inner[:, at]
                SG[ch, pl.ds(j + b, 1)] = terms[:, at]
            return c

        lax.fori_loop(0, 8, pair, 0)
        SG[ch] = SG[ch] / scale

        def send(d, c):
            q = peer(d)
            remote(
                R.at[ch, :, pl.ds(pl.multiple_of(q * 16, 16), 16)], F.at[ch, chip],
                r_send.at[ch], f_sem.at[ch], chip_dev(q),
            ).start()
            return c

        lax.fori_loop(1, CHIPS, send, 0)
        pltpu.make_async_copy(
            R.at[ch, :, pl.ds(pl.multiple_of(chip * 16, 16), 16)], F.at[ch, chip], f_sem.at[ch]
        ).start()
        return carry

    lax.fori_loop(0, CHUNKS, across, 0)

    half_rows = pl.ds(pl.multiple_of(core * 128, 128), 128)
    other_rows = pl.ds(pl.multiple_of(other * 128, 128), 128)

    def sibling_sum_start(k, acc):
        remote(acc.at[other_rows], sib_sum.at[k], sib_send.at[k], sib_sem.at[k], sibling).start()

    def scatter_start(k, acc, extra):
        wait_bytes(sib_sum.at[k], sib_sem.at[k])
        total = acc[half_rows] + sib_sum[k]
        red_send[k, :, 0:8] = total.reshape(CHIPS, 8, LEN)
        red_send[k, :, 8:16] = jnp.zeros((CHIPS, 8, LEN), F32)
        extra()

        def send(d, c):
            q = peer(d)
            remote(red_send.at[k, q], red_recv.at[k, chip], rs_send.at[k], rs_sem.at[k], chip_dev(q)).start()
            return c

        lax.fori_loop(1, CHIPS, send, 0)
        pltpu.make_async_copy(red_send.at[k, chip], red_recv.at[k, chip], rs_sem.at[k]).start()

    def gather_start(k):
        wait_bytes(red_recv.at[k], rs_sem.at[k])
        red_sum[k] = jnp.sum(red_recv[k], axis=0)

        def send(d, c):
            remote(red_sum.at[k], gathered.at[k, chip], ag_send.at[k], ag_sem.at[k], chip_dev(peer(d))).start()
            return c

        lax.fori_loop(1, CHIPS, send, 0)
        pltpu.make_async_copy(red_sum.at[k], gathered.at[k, chip], ag_sem.at[k]).start()

    def swap_start(k):
        wait_bytes(gathered.at[k], ag_sem.at[k])
        remote(gathered.at[k], gathered_sib.at[k], gx_send.at[k], gx_sem.at[k], sibling).start()

    def write_matrix(k, out):
        wait_bytes(gathered_sib.at[k], gx_sem.at[k])
        out[half_rows] = strict_lower(gathered[k, :, 0:8].reshape(128, LEN), core * 128)
        out[other_rows] = strict_lower(gathered_sib[k, :, 0:8].reshape(128, LEN), other * 128)

    def spectrum_start():
        def send(d, c):
            remote(SG, sg_all.at[chip], sg_send, sg_sem, chip_dev(peer(d))).start()
            return c

        lax.fori_loop(1, CHIPS, send, 0)
        pltpu.make_async_copy(SG, sg_all.at[chip], sg_sem).start()

    def spectrum_swap():
        wait_bytes(sg_all, sg_sem)
        remote(sg_all, sg_sib, sgx_send, sgx_sem, sibling).start()

    def spectrum_write():
        wait_bytes(sg_sib, sgx_sem)

        def rows(q, c):
            at = pl.ds(pl.multiple_of(q * 16, 16), 16)
            for ch in range(CHUNKS):
                out_spec[at, lanes_of(core, ch)] = sg_all[q, ch]
                out_spec[at, lanes_of(other, ch)] = sg_sib[q, ch]
            return c

        lax.fori_loop(0, CHIPS, rows, 0)

    def after(ch):
        gt, kt, vt = taps_of(gate_taps, ch), taps_of(key_taps, ch), taps_of(value_taps, ch)
        scale = spectrum[:, lanes_of(core, ch)]
        wait_bytes(F.at[ch], f_sem.at[ch])

        def regroup(j, c):
            rows = F[ch, j].reshape(LEN, 2 * LANES)
            AB[:, pl.ds(pl.multiple_of(j * 16, 16), 16)] = dot(MAT[4], rows).astype(BF16).reshape(
                16, 16, 2 * LANES
            )
            return c

        lax.fori_loop(0, CHIPS, regroup, 0)
        CARRY[...] = jnp.zeros_like(CARRY)

        def pair(step, c):
            p = CHIPS // 2 - 1 - step
            scaled = jnp.concatenate(
                [(AB[2 * p + b, :, LANES:].astype(F32) * scale).astype(BF16) for b in range(2)], 1
            )
            product = jnp.concatenate([PR[ch, block_rows(2 * p + b)] for b in range(2)], 1)
            inner_acc[...] += dot_lanes(scaled, product)
            grad_product = dot(MAT[1], scaled)
            for b in (1, 0):
                i = 2 * p + b
                x = shifted_rows(ch, i)
                gp = grad_product[:, b * LANES:(b + 1) * LANES]
                grads = (
                    CT[ch, block_rows(i)].astype(F32) * AB[i, :, :LANES].astype(F32),
                    gp * conv(vt, x),
                    gp * conv(kt, x),
                )
                for k in range(3):
                    for s in range(3):
                        TA[ch, 3 * k + s] += jnp.sum(
                            (grads[k] * x[s]).reshape(LEN // 8, 8, LANES), axis=0
                        )
                u = [gt[s] * grads[0] + kt[s] * grads[1] + vt[s] * grads[2] for s in range(3)]
                ext1 = jnp.concatenate([u[1], CARRY[0:8]], 0)
                ext2 = jnp.concatenate([u[2], CARRY[8:16]], 0)
                total = u[0] + pltpu.roll(ext1, LEN + 7, 0)[:LEN] + pltpu.roll(ext2, LEN + 6, 0)[:LEN]
                GT[ch, block_rows(i)] = total.astype(BF16)
                CARRY[0:8] = u[1][0:8]
                CARRY[8:16] = u[2][0:8]
                if b == 1:
                    @pl.when(p == CHIPS // 2 - 1)
                    def _():
                        LB[ch] = total[LEN - HALO:]
            return c

        lax.fori_loop(0, CHIPS // 2, pair, 0)
        HB[ch] = CARRY[...]

        @pl.when(chip > 0)
        def _():
            remote(HB.at[ch], HR.at[ch], hb_send.at[ch], hb_sem.at[ch], chip_dev(chip - 1)).start()

    def finish(ch):
        @pl.when(chip < CHIPS - 1)
        def _():
            wait_bytes(HR.at[ch], hb_sem.at[ch])
            row = lax.broadcasted_iota(jnp.int32, (HALO, LANES), 0)
            one, two = HR[ch, 0:8], HR[ch, 8:16]
            last = jnp.where(row == HALO - 1, one[0:1] + two[1:2], jnp.where(row == HALO - 2, two[0:1], 0.0))
            GT[ch, ROWS - HALO:ROWS] = (LB[ch] + last).astype(BF16)

        pltpu.make_async_copy(GT.at[ch, my_rows], out_tok.at[:, lanes_of(core, ch)], out_local.at[ch]).start()
        theirs = pl.ds(pl.multiple_of(other * OWN, OWN), OWN)
        remote(
            GT.at[ch, theirs], out_tok.at[:, lanes_of(core, ch)], out_send.at[ch], out_recv.at[ch], sibling
        ).start()

    sibling_sum_start(0, outer_acc)
    spectrum_start()
    after(0)
    scatter_start(0, outer_acc, lambda: None)
    spectrum_swap()
    after(1)
    finish(0)
    gather_start(0)
    spectrum_write()
    after(2)

    def put_taps():
        for n in range(9 * CHUNKS):
            k, ch = n // CHUNKS, n % CHUNKS
            piece = jnp.sum(TA[ch, k], axis=0, keepdims=True)
            red_send[1, n // 2, 8 + n % 2:9 + n % 2, 0:LANES] = piece

    sibling_sum_start(1, inner_acc)
    finish(1)
    swap_start(0)
    scatter_start(1, inner_acc, put_taps)
    finish(2)
    write_matrix(0, out_outer)
    gather_start(1)
    swap_start(1)
    write_matrix(1, out_inner)
    for n in range(9 * CHUNKS):
        k, ch = n // CHUNKS, n % CHUNKS
        out = (out_gate, out_key, out_value)[k // 3]
        row, at = slice(k % 3, k % 3 + 1), slice(8 + n % 2, 9 + n % 2)
        out[row, lanes_of(core, ch)] = gathered[1, n // 2, at, 0:LANES]
        out[row, lanes_of(other, ch)] = gathered_sib[1, n // 2, at, 0:LANES]

    for ch in range(CHUNKS):
        wait_bytes(T.at[ch, pl.ds(0, OWN)], in_send.at[ch, 0])
        wait_bytes(CT.at[ch, pl.ds(0, OWN)], in_send.at[ch, 1])

        @pl.when(chip < CHIPS - 1)
        def _():
            wait_bytes(T.at[ch, pl.ds(0, HALO)], halo_send.at[ch])

        @pl.when(chip > 0)
        def _():
            wait_bytes(HB.at[ch], hb_send.at[ch])

        wait_bytes(S.at[ch, pl.ds(0, CHIPS - 1)], s_send.at[ch])
        wait_bytes(F.at[ch, pl.ds(0, CHIPS - 1)], r_send.at[ch])
        wait_bytes(GT.at[ch, pl.ds(0, OWN)], out_local.at[ch])
        wait_bytes(GT.at[ch, pl.ds(0, OWN)], out_send.at[ch])
        wait_bytes(GT.at[ch, pl.ds(0, OWN)], out_recv.at[ch])
    for k in range(2):
        wait_bytes(sib_sum.at[k], sib_send.at[k])
        wait_bytes(red_send.at[k, pl.ds(0, CHIPS - 1)], rs_send.at[k])
        wait_bytes(gathered.at[k, pl.ds(0, CHIPS - 1)], ag_send.at[k])
        wait_bytes(gathered.at[k], gx_send.at[k])
    wait_bytes(sg_all.at[pl.ds(0, CHIPS - 1)], sg_send)
    wait_bytes(sg_all, sgx_send)


def body(tokens, cotangent, gate_taps, key_taps, value_taps, inner_mix, outer_mix, spectrum):
    shape = tokens.shape
    channels = shape[2]
    anywhere = pl.BlockSpec(memory_space=pl.ANY)
    vmem = pl.BlockSpec(memory_space=pltpu.VMEM)
    dma = pltpu.SemaphoreType.DMA
    taps_shape = jax.ShapeDtypeStruct((3, channels), F32)
    matrix = jax.ShapeDtypeStruct((LEN, LEN), F32)
    scratch = [
        pltpu.VMEM((CHUNKS, HALO + ROWS, LANES), BF16),
        pltpu.VMEM((CHUNKS, ROWS, LANES), BF16),
        pltpu.VMEM((CHUNKS, ROWS, LANES), BF16),
        pltpu.VMEM((CHIPS, LEN, 2 * LANES), BF16),
        pltpu.VMEM((CHUNKS, CHIPS, 16, 16, 2 * LANES), BF16),
        pltpu.VMEM((CHUNKS, 16, LEN, 2 * LANES), BF16),
        pltpu.VMEM((CHUNKS, 16, LEN, 2 * LANES), BF16),
        pltpu.VMEM((CHUNKS, CHIPS, 16, 16, 2 * LANES), BF16),
        pltpu.VMEM((CHUNKS, ROWS, LANES), BF16),
        pltpu.VMEM((5, LEN, LEN), BF16),
        pltpu.VMEM((16, LANES), F32),
        pltpu.VMEM((CHUNKS, 16, LANES), F32),
        pltpu.VMEM((CHUNKS, 16, LANES), F32),
        pltpu.VMEM((CHUNKS, HALO, LANES), F32),
        pltpu.VMEM((CHUNKS, 9, 8, LANES), F32),
        pltpu.VMEM((LEN, LEN), F32),
        pltpu.VMEM((LEN, LEN), F32),
        pltpu.VMEM((CHUNKS, 16, LANES), F32),
        pltpu.VMEM((2, 128, LEN), F32),
        pltpu.VMEM((2, CHIPS, 16, LEN), F32),
        pltpu.VMEM((2, CHIPS, 16, LEN), F32),
        pltpu.VMEM((2, 16, LEN), F32),
        pltpu.VMEM((2, CHIPS, 16, LEN), F32),
        pltpu.VMEM((2, CHIPS, 16, LEN), F32),
        pltpu.VMEM((CHIPS, CHUNKS, 16, LANES), F32),
        pltpu.VMEM((CHIPS, CHUNKS, 16, LANES), F32),
        dma((CHUNKS, 2)), dma((CHUNKS, 2)),
        dma((CHUNKS,)), dma((CHUNKS,)),
        dma((CHUNKS,)), dma((CHUNKS,)),
        dma((CHUNKS,)), dma((CHUNKS,)),
        dma((CHUNKS,)), dma((CHUNKS,)),
        dma((CHUNKS,)), dma((CHUNKS,)), dma((CHUNKS,)),
        dma((2,)), dma((2,)),
        dma((2,)), dma((2,)),
        dma((2,)), dma((2,)),
        dma((2,)), dma((2,)),
        dma, dma,
        dma, dma,
    ]
    outs = pl.pallas_call(
        kernel,
        out_shape=(
            jax.ShapeDtypeStruct((OWN, channels), BF16),
            taps_shape, taps_shape, taps_shape, matrix, matrix,
            jax.ShapeDtypeStruct((LEN, channels), F32),
        ),
        in_specs=[anywhere] * 2 + [vmem] * 6,
        out_specs=(anywhere,) + (vmem,) * 6,
        scratch_shapes=scratch,
        compiler_params=pltpu.CompilerParams(
            collective_id=0, has_side_effects=True, vmem_limit_bytes=60 * 1024 * 1024
        ),
        cost_estimate=pl.CostEstimate(flops=8 * 10**9, bytes_accessed=12 * 10**6, transcendentals=0),
        name="monarch",
    )(
        tokens.reshape(OWN, channels), cotangent.reshape(OWN, channels),
        gate_taps, key_taps, value_taps, inner_mix, outer_mix, spectrum,
    )
    return (outs[0].reshape(shape),) + tuple(outs[1:])


def solution(mesh):
    in_specs = (
        P(("batch", "seq"), None, None),
        P(("batch", "seq"), None, None),
        P(),
        P(),
        P(),
        P(),
        P(),
        P(),
    )
    out_specs = (
        P(("batch", "seq"), None, None),
        P("batch", None),
        P("batch", None),
        P("batch", None),
        P("batch", None),
        P("batch", None),
        P("batch", None),
    )
    return jax.shard_map(body, mesh=mesh, in_specs=in_specs, out_specs=out_specs, check_vma=False)
```

```python
import jax
import jax.numpy as jnp
from jax import lax
from jax.experimental import pallas as pl
from jax.experimental.pallas import tpu as pltpu
from jax.sharding import PartitionSpec as P

MESH = pl.DeviceIdType.MESH
F32 = jnp.float32
BF16 = jnp.bfloat16

LEN = 256
CHIPS = 16
LANES = 128
CHUNKS = 3
HALF = LANES * CHUNKS
ROWS = CHIPS * LEN
OWN = ROWS // 2
HALO = 16
SUB = 8
SPLIT = 16 // SUB
PER_CHUNK = 4 * SPLIT
UNITS = PER_CHUNK * CHUNKS
AHEAD = 1
TURNS = UNITS // 3
LAGS = (0, 1, 2, 3)
PART = 64
OWN_AT, ONE, TWO, PASS = 0, 1, 2, 3

Y, G = 0, 1
ROUTES = (
    (
        (Y, 1, 0, 1, OWN_AT, ONE, 2), (Y, 1, 1, 2, OWN_AT, ONE, 3), (Y, 2, 1, 2, ONE, TWO, 3), (Y, 3, 2, 3, PASS, ONE, 4),
        (G, 1, 3, 2, OWN_AT, ONE, 2), (G, 1, 2, 1, OWN_AT, ONE, 3), (G, 2, 2, 1, ONE, TWO, 3), (G, 3, 1, 0, PASS, ONE, 4),
    ),
    (
        (Y, 1, 0, 3, OWN_AT, TWO, 2), (Y, 1, 0, 1, OWN_AT, ONE, 4), (Y, 1, 1, 2, OWN_AT, ONE, 3), (Y, 2, 3, 2, TWO, TWO, 3),
        (Y, 3, 2, 3, PASS, ONE, 4),
        (G, 1, 3, 0, OWN_AT, TWO, 2), (G, 1, 3, 2, OWN_AT, ONE, 4), (G, 1, 2, 1, OWN_AT, ONE, 3), (G, 2, 0, 1, TWO, TWO, 3),
        (G, 3, 1, 0, PASS, ONE, 4),
    ),
    (
        (Y, 1, 0, 3, OWN_AT, ONE, 3), (Y, 1, 0, 1, OWN_AT, ONE, 4), (Y, 1, 1, 2, OWN_AT, ONE, 3),
        (Y, 3, 3, 2, PASS, TWO, 4), (Y, 3, 2, 3, PASS, TWO, 4),
        (G, 1, 3, 2, OWN_AT, ONE, 3), (G, 1, 2, 3, OWN_AT, ONE, 3), (G, 1, 1, 0, OWN_AT, ONE, 4),
        (G, 3, 2, 1, PASS, ONE, 4), (G, 3, 3, 0, PASS, TWO, 4),
    ),
)
ROUTE_KIND = (0, 0, 1)
NONE, SUM = -1, -2
OWN_Y = (
    ((0, 1, 2, 3), (0, 1, 2, 3), (NONE, 0, 1, SUM), (NONE, NONE, 0, NONE)),
    ((0, 1, 2, 3), (0, 1, 2, 3), (NONE, 0, 1, 0), (NONE, NONE, SUM, SUM)),
)
PASS_Y = (
    ((0, 0, 3, 0), (NONE, NONE, 2, NONE), (NONE, NONE, 1, NONE), (NONE, NONE, 0, NONE)),
    ((0, 0, 3, 2), (NONE, NONE, 2, NONE), (NONE, NONE, 1, 0), (NONE, NONE, NONE, NONE)),
)
OWN_G = (
    ((0, 1, 2, 3), (0, 1, 2, 3), (SUM, 2, 3, NONE), (NONE, 3, NONE, NONE)),
    ((0, 1, 2, 3), (0, 1, 2, 3), (1, SUM, 3, NONE), (SUM, NONE, NONE, NONE)),
)
PASS_G = (
    ((0, 0, 0, 0), (NONE, 1, NONE, NONE), (NONE, 2, NONE, NONE), (NONE, 3, NONE, NONE)),
    ((0, 0, 1, 0), (NONE, NONE, 2, 3), (NONE, NONE, 3, 2), (NONE, NONE, NONE, NONE)),
)
OUTER_ROWS = (((0, 1, 2, 3), (NONE, NONE, 3, NONE)), ((0, 1, 2, 3), (NONE, NONE, 3, 2)))
OUTER_COLS = (
    (
        ((0, 1, 2, 3), (NONE, 0, 1, NONE), (NONE, NONE, 0, NONE)),
        ((NONE, NONE, 2, NONE), (NONE, NONE, 1, NONE), (NONE, NONE, 0, NONE)),
    ),
    (
        ((0, 1, 2, 3), (NONE, 0, 1, 0), (NONE, NONE, NONE, NONE)),
        ((NONE, NONE, 2, NONE), (NONE, NONE, 1, 0), (NONE, NONE, NONE, NONE)),
    ),
)


def dot(a, b):
    return jnp.dot(a, b, preferred_element_type=F32)


def dot_lanes(a, b):
    return lax.dot_general(a, b, (((1,), (1,)), ((), ())), preferred_element_type=F32)


def strict_lower(value, first_row):
    rows = lax.broadcasted_iota(jnp.int32, value.shape, 0) + first_row
    cols = lax.broadcasted_iota(jnp.int32, value.shape, 1)
    return jnp.where(rows > cols, value, 0.0)


def kernel(
    tok, cot, gate_taps, key_taps, value_taps, inner_mix, outer_mix, spectrum,
    out_tok, out_gate, out_key, out_value, out_inner, out_outer, out_spec,
    T, CT, AB, S, W, PS, F, GT, MAT, MIX, CARRY, HB, HR, LB, TA,
    inner_acc, outer_acc, outer_parts, SGP, SGR, SG, red_send, red_recv, red_sum, red_sib, total, gathered,
    sg_all, sg_sib,
    in_sem, in_send, halo_sem, halo_send, x_sem, x_send, z_sem, z_send, f_sem, r_send, hb_sem, hb_send,
    out_local, out_send, out_recv, sib_sem, sib_send, rs_sem, rs_send, ag_sem, ag_send,
    sp_sem, sp_send, sg_sem, sg_send, sgx_sem, sgx_send,
):
    batch = lax.axis_index("batch")
    seq = lax.axis_index("seq")
    core = seq % 2
    chip = seq // 2
    cz = chip // 4
    cx = chip % 4
    other = 1 - core
    sibling = (batch, chip * 2 + other)

    def chip_dev(q):
        return (batch, q * 2 + core)

    def peer(d):
        return ((cz + d // 4) % 4) * 4 + (cx + d % 4) % 4

    def on_plane(x):
        return chip_dev(cz * 4 + x)

    def at_plane(values):
        out = jnp.int32(values[3])
        for plane in range(3):
            out = jnp.where(cz == plane, jnp.int32(values[plane]), out)
        return out

    def clear(u, carry):
        def rows(j, c):
            W[u, j, PART:] = jnp.zeros((2 * PART, 2 * LANES), BF16)
            return c

        return lax.fori_loop(0, SUB, rows, carry)

    lax.fori_loop(0, UNITS, clear, 0)
    barrier = pltpu.get_barrier_semaphore()

    def greet(d, carry):
        pl.semaphore_signal(barrier, inc=1, device_id=chip_dev(peer(d)), device_id_type=MESH)
        return carry

    lax.fori_loop(1, CHIPS, greet, 0)
    pl.semaphore_signal(barrier, inc=1, device_id=sibling, device_id_type=MESH)
    pl.semaphore_wait(barrier, CHIPS)

    def remote(src, dst, send, recv, device):
        return pltpu.make_async_remote_copy(
            src_ref=src, dst_ref=dst, send_sem=send, recv_sem=recv,
            device_id=device, device_id_type=MESH,
        )

    def wait_bytes(ref, sem):
        pltpu.make_async_copy(ref, ref, sem).wait()

    my_rows = pl.ds(pl.multiple_of(core * OWN, OWN), OWN)
    halo_rows = pl.ds(pl.multiple_of(HALO + core * OWN, HALO), OWN)

    def lanes_of(c, ch):
        return pl.ds(pl.multiple_of(c * HALF + ch * LANES, LANES), LANES)

    def start_inputs(ch, carry):
        remote(tok.at[:, lanes_of(other, ch)], T.at[ch, halo_rows], in_send.at[ch, 0], in_sem.at[ch, 0], sibling).start()
        remote(cot.at[:, lanes_of(other, ch)], CT.at[ch, my_rows], in_send.at[ch, 1], in_sem.at[ch, 1], sibling).start()
        pltpu.make_async_copy(tok.at[:, lanes_of(core, ch)], T.at[ch, halo_rows], in_sem.at[ch, 0]).start()
        pltpu.make_async_copy(cot.at[:, lanes_of(core, ch)], CT.at[ch, my_rows], in_sem.at[ch, 1]).start()
        return carry

    lax.fori_loop(0, CHUNKS, start_inputs, 0)

    row_id = lax.broadcasted_iota(jnp.int32, (LEN, LEN), 0)
    col_id = lax.broadcasted_iota(jnp.int32, (LEN, LEN), 1)
    for at, weights in ((0, inner_mix), (2, outer_mix)):
        full = jnp.where(
            row_id > col_id, weights[...].astype(F32), jnp.where(row_id == col_id, 1.0, 0.0)
        )
        MAT[at] = full.astype(BF16)
        MAT[at + 1] = jnp.transpose(full).astype(BF16)
    MAT[4] = jnp.where(col_id == (row_id % 16) * 16 + row_id // 16, 1.0, 0.0).astype(BF16)
    slot_row = lax.broadcasted_iota(jnp.int32, (LEN, 3 * PART), 0)
    slot_col = lax.broadcasted_iota(jnp.int32, (LEN, 3 * PART), 1)
    eye_row = lax.broadcasted_iota(jnp.int32, (PART, 3 * PART), 0)
    eye_col = lax.broadcasted_iota(jnp.int32, (PART, 3 * PART), 1)
    for kind in range(2):
        for n, (table, mat) in enumerate(((OWN_Y, 2), (PASS_Y, 2), (OWN_G, 3), (PASS_G, 3))):
            to, *slots = table[kind]
            pick = jnp.zeros((LEN, 3 * PART), F32)
            add = jnp.zeros((PART, 3 * PART), F32)
            for k, planes in enumerate(slots):
                plane = at_plane(planes)
                here = jnp.logical_and(slot_col // PART == k, slot_row == plane * PART + slot_col % PART)
                pick = jnp.where(here, 1.0, pick)
                same = jnp.logical_and(eye_col == eye_row + k * PART, plane == SUM)
                add = jnp.where(same, 1.0, add)
            rows = MAT[mat, pl.ds(pl.multiple_of(at_plane(to) * PART, PART), PART)]
            MIX[kind, n] = (dot(rows, pick.astype(BF16)) + add).astype(BF16)
    inner_acc[...] = jnp.zeros_like(inner_acc)
    outer_acc[...] = jnp.zeros_like(outer_acc)
    outer_parts[...] = jnp.zeros_like(outer_parts)
    TA[...] = jnp.zeros_like(TA)

    def send_halo(ch, carry):
        wait_bytes(T.at[ch, pl.ds(HALO, ROWS)], in_sem.at[ch, 0])

        @pl.when(chip < CHIPS - 1)
        def _():
            remote(
                T.at[ch, pl.ds(ROWS, HALO)], T.at[ch, pl.ds(0, HALO)],
                halo_send.at[ch], halo_sem.at[ch], chip_dev(chip + 1),
            ).start()

        @pl.when(chip == 0)
        def _():
            T[ch, 0:HALO] = jnp.zeros((HALO, LANES), BF16)

        wait_bytes(CT.at[ch], in_sem.at[ch, 1])
        return carry

    def taps_of(ref, ch):
        block = ref[:, lanes_of(core, ch)]
        return block[0:1], block[1:2], block[2:3]

    def shifted_rows(ch, i):
        ext = T[ch, pl.ds(pl.multiple_of(i * LEN, LEN), LEN + HALO)].astype(F32)
        return ext[HALO:], pltpu.roll(ext, 1, 0)[HALO:], pltpu.roll(ext, 2, 0)[HALO:]

    def conv(taps, x):
        return taps[0] * x[0] + taps[1] * x[1] + taps[2] * x[2]

    def block_rows(i):
        return pl.ds(pl.multiple_of(i * LEN, LEN), LEN)

    def before(ch, carry):
        gt, kt, vt = taps_of(gate_taps, ch), taps_of(key_taps, ch), taps_of(value_taps, ch)
        send_halo(ch, 0)

        def pair(step, c):
            p = CHIPS // 2 - 1 - step

            @pl.when(jnp.logical_and(p == 0, chip > 0))
            def _():
                wait_bytes(T.at[ch, pl.ds(0, HALO)], halo_sem.at[ch])

            products = []
            for b in range(2):
                i = 2 * p + b
                x = shifted_rows(ch, i)
                product = (conv(kt, x) * conv(vt, x)).astype(BF16)
                products.append(product)
                grad_mixed = CT[ch, block_rows(i)].astype(F32) * conv(gt, x)
                AB[i, :, LANES:] = grad_mixed.astype(BF16)
            pre = dot(MAT[0], jnp.concatenate(products, 1))
            scale = spectrum[:, lanes_of(core, ch)]
            for b in range(2):
                AB[2 * p + b, :, :LANES] = (pre[:, b * LANES:(b + 1) * LANES] * scale).astype(BF16)
            return c

        lax.fori_loop(0, CHIPS // 2, pair, 0)

        def quarter(t, c):
            u0 = ch * PER_CHUNK + t * SPLIT

            def regroup(x, c):
                j = 4 * x + t
                rows = AB[:, pl.ds(pl.multiple_of(j * 16, 16), 16)].reshape(LEN, 2 * LANES)
                made = dot(MAT[4], rows).astype(BF16).reshape(16, 16, 2 * LANES)
                for h in range(SPLIT):
                    S[u0 + h, x] = made[h * SUB:(h + 1) * SUB]
                return c

            lax.fori_loop(0, 4, regroup, 0)

            return c

        lax.fori_loop(0, 4, quarter, 0)
        return carry

    def slot(ref, u, k, array):
        return ref.at[u, :, k * PART:(k + 1) * PART, array * LANES:(array + 1) * LANES]

    def sends(u, route, step):
        for array, when, source, target, here, there, _ in ROUTES[route]:
            if when == step:
                @pl.when(cz == source)
                def _(array=array, target=target, here=here, there=there):
                    origin = slot(PS, u, 0, array) if here == PASS else slot(W, u, here, array)
                    remote(
                        origin, slot(W, u, there, array), z_send.at[u],
                        z_sem.at[u, 2 * array + there - 1], chip_dev(target * 4 + cx),
                    ).start()

    def receives(u, route, step):
        for array, _, _, target, _, there, when in ROUTES[route]:
            if when == step:
                @pl.when(cz == target)
                def _(array=array, there=there):
                    wait_bytes(slot(W, u, there, array), z_sem.at[u, 2 * array + there - 1])

    def pair_of(u, j, array, rows=3 * PART):
        lanes = slice(array * LANES, (array + 1) * LANES)
        return jnp.concatenate([W[u, j, 0:rows, lanes], W[u, j + 1, 0:rows, lanes]], 1)

    def hand_out(u):
        mine = pl.ds(pl.multiple_of(cx * 16, 16), 16)

        def send(d, c):
            x = (cx + d) % 4
            remote(S.at[u, x], W.at[u, :, mine], x_send.at[u], x_sem.at[u], on_plane(x)).start()
            return c

        lax.fori_loop(1, 4, send, 0)
        pltpu.make_async_copy(S.at[u, cx], W.at[u, :, mine], x_sem.at[u]).start()

    def step1(u, route):
        wait_bytes(W.at[u, :, 0:PART], x_sem.at[u])
        sends(u, route, 1)

    def step2(u, route):
        receives(u, route, 2)
        sends(u, route, 2)

    def step3(u, route):
        receives(u, route, 3)
        kind = ROUTE_KIND[route]
        for array in (Y, G):
            single = 2 if array == Y else 1
            used = (3 if kind == 0 else 2) * PART
            passes = cz == single if kind == 0 else cz >= 2

            @pl.when(passes)
            def _(array=array):
                def pair(p, c):
                    j = 2 * p
                    mix = MIX[kind, 2 * array + 1, :, 0:used]
                    total = dot(mix, pair_of(u, j, array, used)).astype(BF16)
                    for b in range(2):
                        PS[u, j + b, :, array * LANES:(array + 1) * LANES] = total[:, b * LANES:(b + 1) * LANES]
                    return c

                lax.fori_loop(0, SUB // 2, pair, 0)
        sends(u, route, 3)

    def step4(u, route):
        receives(u, route, 4)
        kind = ROUTE_KIND[route]
        ch, t, h = u // PER_CHUNK, (u % PER_CHUNK) // SPLIT, u % SPLIT
        back = F.at[ch, 4 * cx + t, pl.ds(h * SUB, SUB)]

        def pair(p, c):
            j = 2 * p
            inner, grads = pair_of(u, j, Y), pair_of(u, j, G)
            mixed = dot(MIX[kind, 0], inner).astype(BF16)
            grad_inner = dot(MIX[kind, 2], grads).astype(BF16)
            outer_parts[kind, :, 0:3 * PART] += dot_lanes(grads[0:2 * PART], inner)
            terms = jnp.sum(
                grad_inner.astype(F32) * inner[0:PART].astype(F32), axis=0, keepdims=True
            )
            for b in range(2):
                at = slice(b * LANES, (b + 1) * LANES)
                S[u, :, j + b, :, :LANES] = mixed[:, at].reshape(4, 16, LANES)
                S[u, :, j + b, :, LANES:] = grad_inner[:, at].reshape(4, 16, LANES)
                SGP[t, ch, pl.ds(h * SUB + j + b, 1)] = terms[:, at]
            return c

        wait_bytes(S.at[u, pl.ds(0, 3)], x_send.at[u])
        lax.fori_loop(0, SUB // 2, pair, 0)

        def send(d, c):
            x = (cx + d) % 4
            remote(
                S.at[u, x], back,
                r_send.at[ch], f_sem.at[ch], on_plane(x),
            ).start()
            return c

        lax.fori_loop(1, 4, send, 0)
        pltpu.make_async_copy(
            S.at[u, cx], back, f_sem.at[ch]
        ).start()

    def place_outer():
        cols = lax.broadcasted_iota(jnp.int32, (PART, LEN), 1)
        for kind in range(2):
            for k in range(2):
                row = at_plane(OUTER_ROWS[kind][k])
                part = outer_parts[kind, k * PART:(k + 1) * PART]
                total = jnp.zeros((PART, LEN), F32)
                for n, planes in enumerate(OUTER_COLS[kind][k]):
                    plane = at_plane(planes)
                    moved = pltpu.roll(part, (plane * PART + LEN - n * PART) % LEN, 1)
                    total = jnp.where(cols // PART == plane, moved, total)

                @pl.when(row != NONE)
                def _(row=row, total=total):
                    outer_acc[pl.ds(pl.multiple_of(row * PART, PART), PART)] += total

    def scatter_start(k, acc, extra):
        red_send[k, :, 0:16] = acc[...].reshape(CHIPS, 16, LEN)
        red_send[k, :, 16:24] = jnp.zeros((CHIPS, 8, LEN), F32)
        extra()

        def send(d, c):
            q = peer(d)
            remote(red_send.at[k, q], red_recv.at[k, chip], rs_send.at[k], rs_sem.at[k], chip_dev(q)).start()
            return c

        lax.fori_loop(1, CHIPS, send, 0)
        pltpu.make_async_copy(red_send.at[k, chip], red_recv.at[k, chip], rs_sem.at[k]).start()

    def swap_start(k):
        wait_bytes(red_recv.at[k], rs_sem.at[k])
        red_sum[k] = jnp.sum(red_recv[k], axis=0)
        remote(red_sum.at[k], red_sib.at[k], sib_send.at[k], sib_sem.at[k], sibling).start()

    def gather_start(k):
        wait_bytes(red_sib.at[k], sib_sem.at[k])
        total[k, 0:16] = red_sum[k, 0:16] + red_sib[k, 0:16]
        total[k, 16:24] = jnp.zeros((8, LEN), F32)
        total[k, pl.ds(16 + core, 1)] = red_sum[k, 16:17]
        total[k, pl.ds(16 + other, 1)] = red_sib[k, 16:17]

        def send(d, c):
            remote(total.at[k], gathered.at[k, chip], ag_send.at[k], ag_sem.at[k], chip_dev(peer(d))).start()
            return c

        lax.fori_loop(1, CHIPS, send, 0)
        pltpu.make_async_copy(total.at[k], gathered.at[k, chip], ag_sem.at[k]).start()

    def write_matrix(k, out):
        wait_bytes(gathered.at[k], ag_sem.at[k])
        out[...] = strict_lower(gathered[k, :, 0:16].reshape(LEN, LEN), 0)

    def spectrum_scatter():
        def send(d, c):
            t = (cz + d) % 4
            remote(SGP.at[t], SGR.at[cz], sp_send, sp_sem, chip_dev(t * 4 + cx)).start()
            return c

        lax.fori_loop(1, 4, send, 0)
        pltpu.make_async_copy(SGP.at[cz], SGR.at[cz], sp_sem).start()

    def spectrum_start():
        wait_bytes(SGR, sp_sem)
        here = pl.ds(pl.multiple_of((4 * cx + cz) * 16, 16), 16)
        for ch in range(CHUNKS):
            SG[ch] = jnp.sum(SGR[:, ch], axis=0) / spectrum[here, lanes_of(core, ch)]

        def send(d, c):
            remote(SG, sg_all.at[chip], sg_send, sg_sem, chip_dev(peer(d))).start()
            return c

        lax.fori_loop(1, CHIPS, send, 0)
        pltpu.make_async_copy(SG, sg_all.at[chip], sg_sem).start()

    def spectrum_swap():
        wait_bytes(sg_all, sg_sem)
        remote(sg_all, sg_sib, sgx_send, sgx_sem, sibling).start()

    def spectrum_write():
        wait_bytes(sg_sib, sgx_sem)

        def rows(q, c):
            at = pl.ds(pl.multiple_of((4 * (q % 4) + q // 4) * 16, 16), 16)
            for ch in range(CHUNKS):
                out_spec[at, lanes_of(core, ch)] = sg_all[q, ch]
                out_spec[at, lanes_of(other, ch)] = sg_sib[q, ch]
            return c

        lax.fori_loop(0, CHIPS, rows, 0)

    def after(ch):
        gt, kt, vt = taps_of(gate_taps, ch), taps_of(key_taps, ch), taps_of(value_taps, ch)
        scale = spectrum[:, lanes_of(core, ch)]
        wait_bytes(F.at[ch], f_sem.at[ch])

        def regroup(j, c):
            rows = F[ch, j].reshape(LEN, 2 * LANES)
            AB[:, pl.ds(pl.multiple_of(j * 16, 16), 16)] = dot(MAT[4], rows).astype(BF16).reshape(
                16, 16, 2 * LANES
            )
            return c

        lax.fori_loop(0, CHIPS, regroup, 0)
        CARRY[...] = jnp.zeros_like(CARRY)

        def pair(step, c):
            p = CHIPS // 2 - 1 - step
            scaled = jnp.concatenate(
                [(AB[2 * p + b, :, LANES:].astype(F32) * scale).astype(BF16) for b in range(2)], 1
            )
            shifts = [shifted_rows(ch, 2 * p + b) for b in range(2)]
            keys = [conv(kt, x) for x in shifts]
            values = [conv(vt, x) for x in shifts]
            product = jnp.concatenate([(keys[b] * values[b]).astype(BF16) for b in range(2)], 1)
            inner_acc[...] += dot_lanes(scaled, product)
            grad_product = dot(MAT[1], scaled)
            for b in (1, 0):
                i = 2 * p + b
                x = shifts[b]
                gp = grad_product[:, b * LANES:(b + 1) * LANES]
                grads = (
                    CT[ch, block_rows(i)].astype(F32) * AB[i, :, :LANES].astype(F32),
                    gp * values[b],
                    gp * keys[b],
                )
                for k in range(3):
                    for s in range(3):
                        TA[ch, 3 * k + s] += jnp.sum(
                            (grads[k] * x[s]).reshape(LEN // 8, 8, LANES), axis=0
                        )
                u = [gt[s] * grads[0] + kt[s] * grads[1] + vt[s] * grads[2] for s in range(3)]
                ext1 = jnp.concatenate([u[1], CARRY[0:8]], 0)
                ext2 = jnp.concatenate([u[2], CARRY[8:16]], 0)
                total = u[0] + pltpu.roll(ext1, LEN + 7, 0)[:LEN] + pltpu.roll(ext2, LEN + 6, 0)[:LEN]
                GT[ch, block_rows(i)] = total.astype(BF16)
                CARRY[0:8] = u[1][0:8]
                CARRY[8:16] = u[2][0:8]
                if b == 1:
                    @pl.when(p == CHIPS // 2 - 1)
                    def _():
                        LB[ch] = total[LEN - HALO:]
            return c

        lax.fori_loop(0, CHIPS // 2, pair, 0)
        HB[ch] = CARRY[...]

        @pl.when(chip > 0)
        def _():
            remote(HB.at[ch], HR.at[ch], hb_send.at[ch], hb_sem.at[ch], chip_dev(chip - 1)).start()

    def finish(ch):
        @pl.when(chip < CHIPS - 1)
        def _():
            wait_bytes(HR.at[ch], hb_sem.at[ch])
            row = lax.broadcasted_iota(jnp.int32, (HALO, LANES), 0)
            one, two = HR[ch, 0:8], HR[ch, 8:16]
            last = jnp.where(row == HALO - 1, one[0:1] + two[1:2], jnp.where(row == HALO - 2, two[0:1], 0.0))
            GT[ch, ROWS - HALO:ROWS] = (LB[ch] + last).astype(BF16)

        pltpu.make_async_copy(GT.at[ch, my_rows], out_tok.at[:, lanes_of(core, ch)], out_local.at[ch]).start()
        theirs = pl.ds(pl.multiple_of(other * OWN, OWN), OWN)
        remote(
            GT.at[ch, theirs], out_tok.at[:, lanes_of(core, ch)], out_send.at[ch], out_recv.at[ch], sibling
        ).start()

    before(0, 0)

    steps = (step1, step2, step3, step4)

    def step(n, k):
        at = k - LAGS[n - 1]

        @pl.when(jnp.logical_and(at >= 0, at < TURNS))
        def _():
            for route in range(len(ROUTES)):
                steps[n - 1](len(ROUTES) * at + route, route)

    def hand_out_turn(at):
        for route in range(len(ROUTES)):
            hand_out(len(ROUTES) * at + route)

    def turn(k, carry):
        @pl.when(k + AHEAD < TURNS)
        def _():
            hand_out_turn(k + AHEAD)

        step(2, k)
        step(3, k)
        step(4, k)
        step(1, k)
        return carry

    for at in range(AHEAD):
        hand_out_turn(at)
    first = -(-PER_CHUNK // len(ROUTES)) + LAGS[3] + 1
    second = -(-2 * PER_CHUNK // len(ROUTES)) + LAGS[3] + 1
    lax.fori_loop(0, 0, turn, 0)
    before(1, 0)
    lax.fori_loop(0, 2, turn, 0)
    before(2, 0)
    lax.fori_loop(2, first, turn, 0)
    after(0)
    lax.fori_loop(first, second, turn, 0)
    after(1)
    finish(0)
    lax.fori_loop(second, TURNS + LAGS[3], turn, 0)
    place_outer()
    scatter_start(0, outer_acc, lambda: None)
    spectrum_scatter()
    after(2)

    def put_taps():
        for n in range(9 * CHUNKS):
            k, ch = n // CHUNKS, n % CHUNKS
            at = slice((n % 2) * LANES, (n % 2 + 1) * LANES)
            red_send[1, n // 2, 16:17, at] = jnp.sum(TA[ch, k], axis=0, keepdims=True)

    scatter_start(1, inner_acc, put_taps)
    swap_start(0)
    spectrum_start()
    finish(1)
    gather_start(0)
    swap_start(1)
    finish(2)
    spectrum_swap()
    gather_start(1)
    write_matrix(0, out_outer)
    spectrum_write()
    write_matrix(1, out_inner)
    for n in range(9 * CHUNKS):
        k, ch = n // CHUNKS, n % CHUNKS
        out = (out_gate, out_key, out_value)[k // 3]
        at = slice((n % 2) * LANES, (n % 2 + 1) * LANES)
        for c in range(2):
            lanes = slice(c * HALF + ch * LANES, c * HALF + (ch + 1) * LANES)
            out[k % 3:k % 3 + 1, lanes] = gathered[1, n // 2, 16 + c:17 + c, at]

    for ch in range(CHUNKS):
        wait_bytes(T.at[ch, pl.ds(0, OWN)], in_send.at[ch, 0])
        wait_bytes(CT.at[ch, pl.ds(0, OWN)], in_send.at[ch, 1])

        @pl.when(chip < CHIPS - 1)
        def _():
            wait_bytes(T.at[ch, pl.ds(0, HALO)], halo_send.at[ch])

        @pl.when(chip > 0)
        def _():
            wait_bytes(HB.at[ch], hb_send.at[ch])

        wait_bytes(F.at[ch, pl.ds(0, 12)], r_send.at[ch])
        wait_bytes(GT.at[ch, pl.ds(0, OWN)], out_local.at[ch])
        wait_bytes(GT.at[ch, pl.ds(0, OWN)], out_send.at[ch])
        wait_bytes(GT.at[ch, pl.ds(0, OWN)], out_recv.at[ch])
    def sent(at, carry):
        for route, lines in enumerate(ROUTES):
            u = len(ROUTES) * at + route
            for source in range(4):
                count = sum(line[2] == source for line in lines)

                @pl.when(cz == source)
                def _(count=count, u=u):
                    wait_bytes(W.at[u, :, 0:count * PART, 0:LANES], z_send.at[u])

        return carry

    lax.fori_loop(0, TURNS, sent, 0)
    for k in range(2):
        wait_bytes(red_sum.at[k], sib_send.at[k])
        wait_bytes(red_send.at[k, pl.ds(0, CHIPS - 1)], rs_send.at[k])
        wait_bytes(gathered.at[k, pl.ds(0, CHIPS - 1)], ag_send.at[k])
    wait_bytes(SGR.at[pl.ds(0, 3)], sp_send)
    wait_bytes(sg_all.at[pl.ds(0, CHIPS - 1)], sg_send)
    wait_bytes(sg_all, sgx_send)


def hand_over(*refs):
    count = (len(refs) - 2) // 3
    held, in_sem, out_sem = refs[2 * count:3 * count], refs[-2], refs[-1]
    pieces = [(0, pl.ds(n * (OWN // 4), OWN // 4)) for n in range(4)]
    pieces += [(n, pl.ds(0, held[n].shape[0])) for n in range(1, count)]
    into = [
        pltpu.make_async_copy(refs[n].at[rows], held[n].at[rows], in_sem.at[k])
        for k, (n, rows) in enumerate(pieces)
    ]
    out = [
        pltpu.make_async_copy(held[n].at[rows], refs[count + n].at[rows], out_sem.at[k])
        for k, (n, rows) in enumerate(pieces)
    ]
    for copy in into:
        copy.start()
    for k, copy in enumerate(out):
        into[k].wait()
        copy.start()
    for copy in out:
        copy.wait()


def body(tokens, cotangent, gate_taps, key_taps, value_taps, inner_mix, outer_mix, spectrum):
    shape = tokens.shape
    channels = shape[2]
    anywhere = pl.BlockSpec(memory_space=pl.ANY)
    vmem = pl.BlockSpec(memory_space=pltpu.VMEM)
    dma = pltpu.SemaphoreType.DMA
    taps_shape = jax.ShapeDtypeStruct((3, channels), F32)
    matrix = jax.ShapeDtypeStruct((LEN, LEN), F32)
    scratch = [
        pltpu.VMEM((CHUNKS, HALO + ROWS, LANES), BF16),
        pltpu.VMEM((CHUNKS, ROWS, LANES), BF16),
        pltpu.VMEM((CHIPS, LEN, 2 * LANES), BF16),
        pltpu.VMEM((UNITS, 4, SUB, 16, 2 * LANES), BF16),
        pltpu.VMEM((UNITS, SUB, 3 * PART, 2 * LANES), BF16),
        pltpu.VMEM((UNITS, SUB, PART, 2 * LANES), BF16),
        pltpu.VMEM((CHUNKS, CHIPS, 16, 16, 2 * LANES), BF16),
        pltpu.VMEM((CHUNKS, ROWS, LANES), BF16),
        pltpu.VMEM((5, LEN, LEN), BF16),
        pltpu.VMEM((2, 4, PART, 3 * PART), BF16),
        pltpu.VMEM((16, LANES), F32),
        pltpu.VMEM((CHUNKS, 16, LANES), F32),
        pltpu.VMEM((CHUNKS, 16, LANES), F32),
        pltpu.VMEM((CHUNKS, HALO, LANES), F32),
        pltpu.VMEM((CHUNKS, 9, 8, LANES), F32),
        pltpu.VMEM((LEN, LEN), F32),
        pltpu.VMEM((LEN, LEN), F32),
        pltpu.VMEM((2, 2 * PART, LEN), F32),
        pltpu.VMEM((4, CHUNKS, 16, LANES), F32),
        pltpu.VMEM((4, CHUNKS, 16, LANES), F32),
        pltpu.VMEM((CHUNKS, 16, LANES), F32),
        pltpu.VMEM((2, CHIPS, 24, LEN), F32),
        pltpu.VMEM((2, CHIPS, 24, LEN), F32),
        pltpu.VMEM((2, 24, LEN), F32),
        pltpu.VMEM((2, 24, LEN), F32),
        pltpu.VMEM((2, 24, LEN), F32),
        pltpu.VMEM((2, CHIPS, 24, LEN), F32),
        pltpu.VMEM((CHIPS, CHUNKS, 16, LANES), F32),
        pltpu.VMEM((CHIPS, CHUNKS, 16, LANES), F32),
        dma((CHUNKS, 2)), dma((CHUNKS, 2)),
        dma((CHUNKS,)), dma((CHUNKS,)),
        dma((UNITS,)), dma((UNITS,)),
        dma((UNITS, 4)), dma((UNITS,)),
        dma((CHUNKS,)), dma((CHUNKS,)),
        dma((CHUNKS,)), dma((CHUNKS,)),
        dma((CHUNKS,)), dma((CHUNKS,)), dma((CHUNKS,)),
        dma((2,)), dma((2,)),
        dma((2,)), dma((2,)),
        dma((2,)), dma((2,)),
        dma, dma,
        dma, dma,
        dma, dma,
    ]
    outs = pl.pallas_call(
        kernel,
        out_shape=(
            jax.ShapeDtypeStruct((OWN, channels), BF16),
            taps_shape, taps_shape, taps_shape, matrix, matrix,
            jax.ShapeDtypeStruct((LEN, channels), F32),
        ),
        in_specs=[anywhere] * 2 + [vmem] * 6,
        out_specs=(anywhere,) + (vmem,) * 6,
        scratch_shapes=scratch,
        compiler_params=pltpu.CompilerParams(
            collective_id=0, has_side_effects=True, vmem_limit_bytes=62 * 1024 * 1024
        ),
        cost_estimate=pl.CostEstimate(flops=8 * 10**9, bytes_accessed=12 * 10**6, transcendentals=0),
        name="monarch",
    )(
        tokens.reshape(OWN, channels), cotangent.reshape(OWN, channels),
        gate_taps, key_taps, value_taps, inner_mix, outer_mix, spectrum,
    )
    outs = pl.pallas_call(
        hand_over,
        out_shape=tuple(jax.ShapeDtypeStruct(out.shape, out.dtype) for out in outs),
        in_specs=[anywhere] * len(outs),
        out_specs=(anywhere,) * len(outs),
        scratch_shapes=[pltpu.VMEM(out.shape, out.dtype) for out in outs] + [dma((10,)), dma((10,))],
        name="results",
    )(*outs)
    return (outs[0].reshape(shape),) + tuple(outs[1:])


def solution(mesh):
    in_specs = (
        P(("batch", "seq"), None, None),
        P(("batch", "seq"), None, None),
        P(),
        P(),
        P(),
        P(),
        P(),
        P(),
    )
    out_specs = (
        P(("batch", "seq"), None, None),
        P("batch", None),
        P("batch", None),
        P("batch", None),
        P("batch", None),
        P("batch", None),
        P("batch", None),
    )
    return jax.shard_map(body, mesh=mesh, in_specs=in_specs, out_specs=out_specs, check_vma=False)
```

```python
import jax
import jax.numpy as jnp
from jax import lax
from jax.experimental import pallas as pl
from jax.experimental.pallas import tpu as pltpu
from jax.sharding import PartitionSpec as P

MESH = pl.DeviceIdType.MESH
F32 = jnp.float32
BF16 = jnp.bfloat16

LEN = 256
CHIPS = 16
LANES = 128
CHUNKS = 3
HALF = LANES * CHUNKS
ROWS = CHIPS * LEN
OWN = ROWS // 2
HALO = 16
SUB = 8
SPLIT = 16 // SUB
PER_CHUNK = 4 * SPLIT
UNITS = PER_CHUNK * CHUNKS
AHEAD = 1
TURNS = UNITS // 3
LAGS = (0, 1, 2, 3)
PART = 64
OWN_AT, ONE, TWO, PASS = 0, 1, 2, 3

Y, G = 0, 1
ROUTES = (
    (
        (Y, 1, 0, 1, OWN_AT, ONE, 2), (Y, 1, 1, 2, OWN_AT, ONE, 3), (Y, 2, 1, 2, ONE, TWO, 3), (Y, 3, 2, 3, PASS, ONE, 4),
        (G, 1, 3, 2, OWN_AT, ONE, 2), (G, 1, 2, 1, OWN_AT, ONE, 3), (G, 2, 2, 1, ONE, TWO, 3), (G, 3, 1, 0, PASS, ONE, 4),
    ),
    (
        (Y, 1, 0, 3, OWN_AT, TWO, 2), (Y, 1, 0, 1, OWN_AT, ONE, 4), (Y, 1, 1, 2, OWN_AT, ONE, 3), (Y, 2, 3, 2, TWO, TWO, 3),
        (Y, 3, 2, 3, PASS, ONE, 4),
        (G, 1, 3, 0, OWN_AT, TWO, 2), (G, 1, 3, 2, OWN_AT, ONE, 4), (G, 1, 2, 1, OWN_AT, ONE, 3), (G, 2, 0, 1, TWO, TWO, 3),
        (G, 3, 1, 0, PASS, ONE, 4),
    ),
    (
        (Y, 1, 0, 3, OWN_AT, ONE, 3), (Y, 1, 0, 1, OWN_AT, ONE, 4), (Y, 1, 1, 2, OWN_AT, ONE, 3),
        (Y, 3, 3, 2, PASS, TWO, 4), (Y, 3, 2, 3, PASS, TWO, 4),
        (G, 1, 3, 2, OWN_AT, ONE, 3), (G, 1, 2, 3, OWN_AT, ONE, 3), (G, 1, 1, 0, OWN_AT, ONE, 4),
        (G, 3, 2, 1, PASS, ONE, 4), (G, 3, 3, 0, PASS, TWO, 4),
    ),
)
ROUTE_KIND = (0, 0, 1)
NONE, SUM = -1, -2
OWN_Y = (
    ((0, 1, 2, 3), (0, 1, 2, 3), (NONE, 0, 1, SUM), (NONE, NONE, 0, NONE)),
    ((0, 1, 2, 3), (0, 1, 2, 3), (NONE, 0, 1, 0), (NONE, NONE, SUM, SUM)),
)
PASS_Y = (
    ((0, 0, 3, 0), (NONE, NONE, 2, NONE), (NONE, NONE, 1, NONE), (NONE, NONE, 0, NONE)),
    ((0, 0, 3, 2), (NONE, NONE, 2, NONE), (NONE, NONE, 1, 0), (NONE, NONE, NONE, NONE)),
)
OWN_G = (
    ((0, 1, 2, 3), (0, 1, 2, 3), (SUM, 2, 3, NONE), (NONE, 3, NONE, NONE)),
    ((0, 1, 2, 3), (0, 1, 2, 3), (1, SUM, 3, NONE), (SUM, NONE, NONE, NONE)),
)
PASS_G = (
    ((0, 0, 0, 0), (NONE, 1, NONE, NONE), (NONE, 2, NONE, NONE), (NONE, 3, NONE, NONE)),
    ((0, 0, 1, 0), (NONE, NONE, 2, 3), (NONE, NONE, 3, 2), (NONE, NONE, NONE, NONE)),
)
OUTER_ROWS = (((0, 1, 2, 3), (NONE, NONE, 3, NONE)), ((0, 1, 2, 3), (NONE, NONE, 3, 2)))
OUTER_COLS = (
    (
        ((0, 1, 2, 3), (NONE, 0, 1, NONE), (NONE, NONE, 0, NONE)),
        ((NONE, NONE, 2, NONE), (NONE, NONE, 1, NONE), (NONE, NONE, 0, NONE)),
    ),
    (
        ((0, 1, 2, 3), (NONE, 0, 1, 0), (NONE, NONE, NONE, NONE)),
        ((NONE, NONE, 2, NONE), (NONE, NONE, 1, 0), (NONE, NONE, NONE, NONE)),
    ),
)


def dot(a, b):
    return jnp.dot(a, b, preferred_element_type=F32)


def dot_lanes(a, b):
    return lax.dot_general(a, b, (((1,), (1,)), ((), ())), preferred_element_type=F32)


def strict_lower(value, first_row):
    rows = lax.broadcasted_iota(jnp.int32, value.shape, 0) + first_row
    cols = lax.broadcasted_iota(jnp.int32, value.shape, 1)
    return jnp.where(rows > cols, value, 0.0)


def kernel(
    tok, cot, gate_taps, key_taps, value_taps, inner_mix, outer_mix, spectrum,
    out_tok, out_gate, out_key, out_value, out_inner, out_outer, out_spec,
    T, CT, AB, S, W, PS, F, GT, MAT, MIX, CARRY, HB, HR, LB, TA,
    inner_acc, outer_acc, outer_parts, SGP, SGR, SG, red_send, red_recv, red_sum, red_sib, total, gathered,
    sg_all, sg_sib,
    in_sem, in_send, halo_sem, halo_send, x_sem, x_send, z_sem, z_send, f_sem, r_send, hb_sem, hb_send,
    out_local, out_send, out_recv, sib_sem, sib_send, rs_sem, rs_send, ag_sem, ag_send,
    sp_sem, sp_send, sg_sem, sg_send, sgx_sem, sgx_send,
):
    batch = lax.axis_index("batch")
    seq = lax.axis_index("seq")
    core = seq % 2
    chip = seq // 2
    cz = chip // 4
    cx = chip % 4
    other = 1 - core
    sibling = (batch, chip * 2 + other)

    def chip_dev(q):
        return (batch, q * 2 + core)

    def peer(d):
        return ((cz + d // 4) % 4) * 4 + (cx + d % 4) % 4

    def on_plane(x):
        return chip_dev(cz * 4 + x)

    def at_plane(values):
        out = jnp.int32(values[3])
        for plane in range(3):
            out = jnp.where(cz == plane, jnp.int32(values[plane]), out)
        return out

    def clear(u, carry):
        def rows(j, c):
            W[u, j, PART:] = jnp.zeros((2 * PART, 2 * LANES), BF16)
            return c

        return lax.fori_loop(0, SUB, rows, carry)

    lax.fori_loop(0, UNITS, clear, 0)
    barrier = pltpu.get_barrier_semaphore()

    def greet(d, carry):
        pl.semaphore_signal(barrier, inc=1, device_id=chip_dev(peer(d)), device_id_type=MESH)
        return carry

    lax.fori_loop(1, CHIPS, greet, 0)
    pl.semaphore_signal(barrier, inc=1, device_id=sibling, device_id_type=MESH)
    pl.semaphore_wait(barrier, CHIPS)

    def remote(src, dst, send, recv, device):
        return pltpu.make_async_remote_copy(
            src_ref=src, dst_ref=dst, send_sem=send, recv_sem=recv,
            device_id=device, device_id_type=MESH,
        )

    def wait_bytes(ref, sem):
        pltpu.make_async_copy(ref, ref, sem).wait()

    my_rows = pl.ds(pl.multiple_of(core * OWN, OWN), OWN)
    halo_rows = pl.ds(pl.multiple_of(HALO + core * OWN, HALO), OWN)

    def lanes_of(c, ch):
        return pl.ds(pl.multiple_of(c * HALF + ch * LANES, LANES), LANES)

    def start_inputs(ch, carry):
        remote(tok.at[:, lanes_of(other, ch)], T.at[ch, halo_rows], in_send.at[ch, 0], in_sem.at[ch, 0], sibling).start()
        remote(cot.at[:, lanes_of(other, ch)], CT.at[ch, my_rows], in_send.at[ch, 1], in_sem.at[ch, 1], sibling).start()
        pltpu.make_async_copy(tok.at[:, lanes_of(core, ch)], T.at[ch, halo_rows], in_sem.at[ch, 0]).start()
        pltpu.make_async_copy(cot.at[:, lanes_of(core, ch)], CT.at[ch, my_rows], in_sem.at[ch, 1]).start()
        return carry

    lax.fori_loop(0, CHUNKS, start_inputs, 0)

    row_id = lax.broadcasted_iota(jnp.int32, (LEN, LEN), 0)
    col_id = lax.broadcasted_iota(jnp.int32, (LEN, LEN), 1)
    for at, weights in ((0, inner_mix), (2, outer_mix)):
        full = jnp.where(
            row_id > col_id, weights[...].astype(F32), jnp.where(row_id == col_id, 1.0, 0.0)
        )
        MAT[at] = full.astype(BF16)
        MAT[at + 1] = jnp.transpose(full).astype(BF16)
    MAT[4] = jnp.where(col_id == (row_id % 16) * 16 + row_id // 16, 1.0, 0.0).astype(BF16)
    slot_row = lax.broadcasted_iota(jnp.int32, (LEN, 3 * PART), 0)
    slot_col = lax.broadcasted_iota(jnp.int32, (LEN, 3 * PART), 1)
    eye_row = lax.broadcasted_iota(jnp.int32, (PART, 3 * PART), 0)
    eye_col = lax.broadcasted_iota(jnp.int32, (PART, 3 * PART), 1)
    for kind in range(2):
        for n, (table, mat) in enumerate(((OWN_Y, 2), (PASS_Y, 2), (OWN_G, 3), (PASS_G, 3))):
            to, *slots = table[kind]
            pick = jnp.zeros((LEN, 3 * PART), F32)
            add = jnp.zeros((PART, 3 * PART), F32)
            for k, planes in enumerate(slots):
                plane = at_plane(planes)
                here = jnp.logical_and(slot_col // PART == k, slot_row == plane * PART + slot_col % PART)
                pick = jnp.where(here, 1.0, pick)
                same = jnp.logical_and(eye_col == eye_row + k * PART, plane == SUM)
                add = jnp.where(same, 1.0, add)
            rows = MAT[mat, pl.ds(pl.multiple_of(at_plane(to) * PART, PART), PART)]
            MIX[kind, n] = (dot(rows, pick.astype(BF16)) + add).astype(BF16)
    inner_acc[...] = jnp.zeros_like(inner_acc)
    outer_acc[...] = jnp.zeros_like(outer_acc)
    outer_parts[...] = jnp.zeros_like(outer_parts)
    TA[...] = jnp.zeros_like(TA)

    def send_halo(ch, carry):
        wait_bytes(T.at[ch, pl.ds(HALO, ROWS)], in_sem.at[ch, 0])

        @pl.when(chip < CHIPS - 1)
        def _():
            remote(
                T.at[ch, pl.ds(ROWS, HALO)], T.at[ch, pl.ds(0, HALO)],
                halo_send.at[ch], halo_sem.at[ch], chip_dev(chip + 1),
            ).start()

        @pl.when(chip == 0)
        def _():
            T[ch, 0:HALO] = jnp.zeros((HALO, LANES), BF16)

        wait_bytes(CT.at[ch], in_sem.at[ch, 1])
        return carry

    def taps_of(ref, ch):
        block = ref[:, lanes_of(core, ch)]
        return block[0:1], block[1:2], block[2:3]

    def shifted_rows(ch, i):
        ext = T[ch, pl.ds(pl.multiple_of(i * LEN, LEN), LEN + HALO)].astype(F32)
        return ext[HALO:], pltpu.roll(ext, 1, 0)[HALO:], pltpu.roll(ext, 2, 0)[HALO:]

    def conv(taps, x):
        return taps[0] * x[0] + taps[1] * x[1] + taps[2] * x[2]

    def block_rows(i):
        return pl.ds(pl.multiple_of(i * LEN, LEN), LEN)

    def before(ch, carry):
        gt, kt, vt = taps_of(gate_taps, ch), taps_of(key_taps, ch), taps_of(value_taps, ch)
        send_halo(ch, 0)

        def pair(step, c):
            p = CHIPS // 2 - 1 - step

            @pl.when(jnp.logical_and(p == 0, chip > 0))
            def _():
                wait_bytes(T.at[ch, pl.ds(0, HALO)], halo_sem.at[ch])

            products = []
            for b in range(2):
                i = 2 * p + b
                x = shifted_rows(ch, i)
                product = (conv(kt, x) * conv(vt, x)).astype(BF16)
                products.append(product)
                grad_mixed = CT[ch, block_rows(i)].astype(F32) * conv(gt, x)
                AB[i, :, LANES:] = grad_mixed.astype(BF16)
            pre = dot(MAT[0], jnp.concatenate(products, 1))
            scale = spectrum[:, lanes_of(core, ch)]
            for b in range(2):
                AB[2 * p + b, :, :LANES] = (pre[:, b * LANES:(b + 1) * LANES] * scale).astype(BF16)
            return c

        lax.fori_loop(0, CHIPS // 2, pair, 0)

        def quarter(t, c):
            u0 = ch * PER_CHUNK + t * SPLIT

            def regroup(x, c):
                j = 4 * x + t
                rows = AB[:, pl.ds(pl.multiple_of(j * 16, 16), 16)].reshape(LEN, 2 * LANES)
                made = dot(MAT[4], rows).astype(BF16).reshape(16, 16, 2 * LANES)
                for h in range(SPLIT):
                    S[u0 + h, x] = made[h * SUB:(h + 1) * SUB]
                return c

            lax.fori_loop(0, 4, regroup, 0)

            return c

        lax.fori_loop(0, 4, quarter, 0)
        return carry

    def slot(ref, u, k, array):
        return ref.at[u, :, k * PART:(k + 1) * PART, array * LANES:(array + 1) * LANES]

    def sends(u, route, step):
        for array, when, source, target, here, there, _ in ROUTES[route]:
            if when == step:
                @pl.when(cz == source)
                def _(array=array, target=target, here=here, there=there):
                    origin = slot(PS, u, 0, array) if here == PASS else slot(W, u, here, array)
                    remote(
                        origin, slot(W, u, there, array), z_send.at[u],
                        z_sem.at[u, 2 * array + there - 1], chip_dev(target * 4 + cx),
                    ).start()

    def receives(u, route, step):
        for array, _, _, target, _, there, when in ROUTES[route]:
            if when == step:
                @pl.when(cz == target)
                def _(array=array, there=there):
                    wait_bytes(slot(W, u, there, array), z_sem.at[u, 2 * array + there - 1])

    def pair_of(u, j, array, rows=3 * PART):
        lanes = slice(array * LANES, (array + 1) * LANES)
        return jnp.concatenate([W[u, j, 0:rows, lanes], W[u, j + 1, 0:rows, lanes]], 1)

    def hand_out(u):
        mine = pl.ds(pl.multiple_of(cx * 16, 16), 16)

        def send(d, c):
            x = (cx + d) % 4
            remote(S.at[u, x], W.at[u, :, mine], x_send.at[u], x_sem.at[u], on_plane(x)).start()
            return c

        lax.fori_loop(1, 4, send, 0)
        pltpu.make_async_copy(S.at[u, cx], W.at[u, :, mine], x_sem.at[u]).start()

    def step1(u, route):
        wait_bytes(W.at[u, :, 0:PART], x_sem.at[u])
        sends(u, route, 1)

    def step2(u, route):
        receives(u, route, 2)
        sends(u, route, 2)

    def step3(u, route):
        receives(u, route, 3)
        kind = ROUTE_KIND[route]
        for array in (Y, G):
            single = 2 if array == Y else 1
            used = (3 if kind == 0 else 2) * PART
            passes = cz == single if kind == 0 else cz >= 2

            @pl.when(passes)
            def _(array=array):
                def pair(p, c):
                    j = 2 * p
                    mix = MIX[kind, 2 * array + 1, :, 0:used]
                    total = dot(mix, pair_of(u, j, array, used)).astype(BF16)
                    for b in range(2):
                        PS[u, j + b, :, array * LANES:(array + 1) * LANES] = total[:, b * LANES:(b + 1) * LANES]
                    return c

                lax.fori_loop(0, SUB // 2, pair, 0)
        sends(u, route, 3)

    def step4(u, route):
        receives(u, route, 4)
        kind = ROUTE_KIND[route]
        ch, t, h = u // PER_CHUNK, (u % PER_CHUNK) // SPLIT, u % SPLIT
        back = F.at[ch, 4 * cx + t, pl.ds(h * SUB, SUB)]

        def pair(p, c):
            j = 2 * p
            inner, grads = pair_of(u, j, Y), pair_of(u, j, G)
            mixed = dot(MIX[kind, 0], inner).astype(BF16)
            grad_inner = dot(MIX[kind, 2], grads).astype(BF16)
            outer_parts[kind, :, 0:3 * PART] += dot_lanes(grads[0:2 * PART], inner)
            terms = jnp.sum(
                grad_inner.astype(F32) * inner[0:PART].astype(F32), axis=0, keepdims=True
            )
            for b in range(2):
                at = slice(b * LANES, (b + 1) * LANES)
                S[u, :, j + b, :, :LANES] = mixed[:, at].reshape(4, 16, LANES)
                S[u, :, j + b, :, LANES:] = grad_inner[:, at].reshape(4, 16, LANES)
                SGP[t, ch, pl.ds(h * SUB + j + b, 1)] = terms[:, at]
            return c

        wait_bytes(S.at[u, pl.ds(0, 3)], x_send.at[u])
        lax.fori_loop(0, SUB // 2, pair, 0)

        def send(d, c):
            x = (cx + d) % 4
            remote(
                S.at[u, x], back,
                r_send.at[ch], f_sem.at[ch], on_plane(x),
            ).start()
            return c

        lax.fori_loop(1, 4, send, 0)
        pltpu.make_async_copy(
            S.at[u, cx], back, f_sem.at[ch]
        ).start()

    def place_outer():
        cols = lax.broadcasted_iota(jnp.int32, (PART, LEN), 1)
        for kind in range(2):
            for k in range(2):
                row = at_plane(OUTER_ROWS[kind][k])
                part = outer_parts[kind, k * PART:(k + 1) * PART]
                total = jnp.zeros((PART, LEN), F32)
                for n, planes in enumerate(OUTER_COLS[kind][k]):
                    plane = at_plane(planes)
                    moved = pltpu.roll(part, (plane * PART + LEN - n * PART) % LEN, 1)
                    total = jnp.where(cols // PART == plane, moved, total)

                @pl.when(row != NONE)
                def _(row=row, total=total):
                    outer_acc[pl.ds(pl.multiple_of(row * PART, PART), PART)] += total

    def scatter_start(k, acc, extra):
        red_send[k, :, 0:16] = acc[...].reshape(CHIPS, 16, LEN)
        red_send[k, :, 16:24] = jnp.zeros((CHIPS, 8, LEN), F32)
        extra()

        def send(d, c):
            q = peer(d)
            remote(red_send.at[k, q], red_recv.at[k, chip], rs_send.at[k], rs_sem.at[k], chip_dev(q)).start()
            return c

        lax.fori_loop(1, CHIPS, send, 0)
        pltpu.make_async_copy(red_send.at[k, chip], red_recv.at[k, chip], rs_sem.at[k]).start()

    def swap_start(k):
        wait_bytes(red_recv.at[k], rs_sem.at[k])
        red_sum[k] = jnp.sum(red_recv[k], axis=0)
        remote(red_sum.at[k], red_sib.at[k], sib_send.at[k], sib_sem.at[k], sibling).start()

    def gather_start(k):
        wait_bytes(red_sib.at[k], sib_sem.at[k])
        total[k, 0:16] = red_sum[k, 0:16] + red_sib[k, 0:16]
        total[k, 16:24] = jnp.zeros((8, LEN), F32)
        total[k, pl.ds(16 + core, 1)] = red_sum[k, 16:17]
        total[k, pl.ds(16 + other, 1)] = red_sib[k, 16:17]

        def send(d, c):
            remote(total.at[k], gathered.at[k, chip], ag_send.at[k], ag_sem.at[k], chip_dev(peer(d))).start()
            return c

        lax.fori_loop(1, CHIPS, send, 0)
        pltpu.make_async_copy(total.at[k], gathered.at[k, chip], ag_sem.at[k]).start()

    def write_matrix(k, out):
        wait_bytes(gathered.at[k], ag_sem.at[k])
        out[...] = strict_lower(gathered[k, :, 0:16].reshape(LEN, LEN), 0)

    def spectrum_scatter():
        def send(d, c):
            t = (cz + d) % 4
            remote(SGP.at[t], SGR.at[cz], sp_send, sp_sem, chip_dev(t * 4 + cx)).start()
            return c

        lax.fori_loop(1, 4, send, 0)
        pltpu.make_async_copy(SGP.at[cz], SGR.at[cz], sp_sem).start()

    def spectrum_start():
        wait_bytes(SGR, sp_sem)
        here = pl.ds(pl.multiple_of((4 * cx + cz) * 16, 16), 16)
        for ch in range(CHUNKS):
            SG[ch] = jnp.sum(SGR[:, ch], axis=0) / spectrum[here, lanes_of(core, ch)]

        def send(d, c):
            remote(SG, sg_all.at[chip], sg_send, sg_sem, chip_dev(peer(d))).start()
            return c

        lax.fori_loop(1, CHIPS, send, 0)
        pltpu.make_async_copy(SG, sg_all.at[chip], sg_sem).start()

    def spectrum_swap():
        wait_bytes(sg_all, sg_sem)
        remote(sg_all, sg_sib, sgx_send, sgx_sem, sibling).start()

    def spectrum_write():
        wait_bytes(sg_sib, sgx_sem)

        def rows(q, c):
            at = pl.ds(pl.multiple_of((4 * (q % 4) + q // 4) * 16, 16), 16)
            for ch in range(CHUNKS):
                out_spec[at, lanes_of(core, ch)] = sg_all[q, ch]
                out_spec[at, lanes_of(other, ch)] = sg_sib[q, ch]
            return c

        lax.fori_loop(0, CHIPS, rows, 0)

    def after(ch):
        gt, kt, vt = taps_of(gate_taps, ch), taps_of(key_taps, ch), taps_of(value_taps, ch)
        scale = spectrum[:, lanes_of(core, ch)]
        wait_bytes(F.at[ch], f_sem.at[ch])

        def regroup(j, c):
            rows = F[ch, j].reshape(LEN, 2 * LANES)
            AB[:, pl.ds(pl.multiple_of(j * 16, 16), 16)] = dot(MAT[4], rows).astype(BF16).reshape(
                16, 16, 2 * LANES
            )
            return c

        lax.fori_loop(0, CHIPS, regroup, 0)
        CARRY[...] = jnp.zeros_like(CARRY)

        def pair(step, c):
            p = CHIPS // 2 - 1 - step
            scaled = jnp.concatenate(
                [(AB[2 * p + b, :, LANES:].astype(F32) * scale).astype(BF16) for b in range(2)], 1
            )
            shifts = [shifted_rows(ch, 2 * p + b) for b in range(2)]
            keys = [conv(kt, x) for x in shifts]
            values = [conv(vt, x) for x in shifts]
            product = jnp.concatenate([(keys[b] * values[b]).astype(BF16) for b in range(2)], 1)
            inner_acc[...] += dot_lanes(scaled, product)
            grad_product = dot(MAT[1], scaled)
            for b in (1, 0):
                i = 2 * p + b
                x = shifts[b]
                gp = grad_product[:, b * LANES:(b + 1) * LANES]
                grads = (
                    CT[ch, block_rows(i)].astype(F32) * AB[i, :, :LANES].astype(F32),
                    gp * values[b],
                    gp * keys[b],
                )
                for k in range(3):
                    for s in range(3):
                        TA[ch, 3 * k + s] += jnp.sum(
                            (grads[k] * x[s]).reshape(LEN // 8, 8, LANES), axis=0
                        )
                u = [gt[s] * grads[0] + kt[s] * grads[1] + vt[s] * grads[2] for s in range(3)]
                ext1 = jnp.concatenate([u[1], CARRY[0:8]], 0)
                ext2 = jnp.concatenate([u[2], CARRY[8:16]], 0)
                total = u[0] + pltpu.roll(ext1, LEN + 7, 0)[:LEN] + pltpu.roll(ext2, LEN + 6, 0)[:LEN]
                GT[ch, block_rows(i)] = total.astype(BF16)
                CARRY[0:8] = u[1][0:8]
                CARRY[8:16] = u[2][0:8]
                if b == 1:
                    @pl.when(p == CHIPS // 2 - 1)
                    def _():
                        LB[ch] = total[LEN - HALO:]
            return c

        lax.fori_loop(0, CHIPS // 2, pair, 0)
        HB[ch] = CARRY[...]

        @pl.when(chip > 0)
        def _():
            remote(HB.at[ch], HR.at[ch], hb_send.at[ch], hb_sem.at[ch], chip_dev(chip - 1)).start()

    def finish(ch):
        @pl.when(chip < CHIPS - 1)
        def _():
            wait_bytes(HR.at[ch], hb_sem.at[ch])
            row = lax.broadcasted_iota(jnp.int32, (HALO, LANES), 0)
            one, two = HR[ch, 0:8], HR[ch, 8:16]
            last = jnp.where(row == HALO - 1, one[0:1] + two[1:2], jnp.where(row == HALO - 2, two[0:1], 0.0))
            GT[ch, ROWS - HALO:ROWS] = (LB[ch] + last).astype(BF16)

        pltpu.make_async_copy(GT.at[ch, my_rows], out_tok.at[:, lanes_of(core, ch)], out_local.at[ch]).start()
        theirs = pl.ds(pl.multiple_of(other * OWN, OWN), OWN)
        remote(
            GT.at[ch, theirs], out_tok.at[:, lanes_of(core, ch)], out_send.at[ch], out_recv.at[ch], sibling
        ).start()

    before(0, 0)

    steps = (step1, step2, step3, step4)

    def step(n, k):
        at = k - LAGS[n - 1]

        @pl.when(jnp.logical_and(at >= 0, at < TURNS))
        def _():
            for route in range(len(ROUTES)):
                steps[n - 1](len(ROUTES) * at + route, route)

    def hand_out_turn(at):
        for route in range(len(ROUTES)):
            hand_out(len(ROUTES) * at + route)

    def turn(k, carry):
        @pl.when(k + AHEAD < TURNS)
        def _():
            hand_out_turn(k + AHEAD)

        step(2, k)
        step(3, k)
        step(4, k)
        step(1, k)
        return carry

    for at in range(AHEAD):
        hand_out_turn(at)
    first = -(-PER_CHUNK // len(ROUTES)) + LAGS[3] + 0
    second = -(-2 * PER_CHUNK // len(ROUTES)) + LAGS[3] + 0
    lax.fori_loop(0, 0, turn, 0)
    before(1, 0)
    lax.fori_loop(0, 2, turn, 0)
    before(2, 0)
    lax.fori_loop(2, first, turn, 0)
    after(0)
    lax.fori_loop(first, second, turn, 0)
    after(1)
    finish(0)
    lax.fori_loop(second, TURNS + LAGS[3], turn, 0)
    place_outer()
    scatter_start(0, outer_acc, lambda: None)
    spectrum_scatter()
    after(2)

    def put_taps():
        for n in range(9 * CHUNKS):
            k, ch = n // CHUNKS, n % CHUNKS
            at = slice((n % 2) * LANES, (n % 2 + 1) * LANES)
            red_send[1, n // 2, 16:17, at] = jnp.sum(TA[ch, k], axis=0, keepdims=True)

    scatter_start(1, inner_acc, put_taps)
    swap_start(0)
    spectrum_start()
    finish(1)
    gather_start(0)
    swap_start(1)
    finish(2)
    spectrum_swap()
    gather_start(1)
    write_matrix(0, out_outer)
    spectrum_write()
    write_matrix(1, out_inner)
    for n in range(9 * CHUNKS):
        k, ch = n // CHUNKS, n % CHUNKS
        out = (out_gate, out_key, out_value)[k // 3]
        at = slice((n % 2) * LANES, (n % 2 + 1) * LANES)
        for c in range(2):
            lanes = slice(c * HALF + ch * LANES, c * HALF + (ch + 1) * LANES)
            out[k % 3:k % 3 + 1, lanes] = gathered[1, n // 2, 16 + c:17 + c, at]

    for ch in range(CHUNKS):
        wait_bytes(T.at[ch, pl.ds(0, OWN)], in_send.at[ch, 0])
        wait_bytes(CT.at[ch, pl.ds(0, OWN)], in_send.at[ch, 1])

        @pl.when(chip < CHIPS - 1)
        def _():
            wait_bytes(T.at[ch, pl.ds(0, HALO)], halo_send.at[ch])

        @pl.when(chip > 0)
        def _():
            wait_bytes(HB.at[ch], hb_send.at[ch])

        wait_bytes(F.at[ch, pl.ds(0, 12)], r_send.at[ch])
        wait_bytes(GT.at[ch, pl.ds(0, OWN)], out_local.at[ch])
        wait_bytes(GT.at[ch, pl.ds(0, OWN)], out_send.at[ch])
        wait_bytes(GT.at[ch, pl.ds(0, OWN)], out_recv.at[ch])
    def sent(at, carry):
        for route, lines in enumerate(ROUTES):
            u = len(ROUTES) * at + route
            for source in range(4):
                count = sum(line[2] == source for line in lines)

                @pl.when(cz == source)
                def _(count=count, u=u):
                    wait_bytes(W.at[u, :, 0:count * PART, 0:LANES], z_send.at[u])

        return carry

    lax.fori_loop(0, TURNS, sent, 0)
    for k in range(2):
        wait_bytes(red_sum.at[k], sib_send.at[k])
        wait_bytes(red_send.at[k, pl.ds(0, CHIPS - 1)], rs_send.at[k])
        wait_bytes(gathered.at[k, pl.ds(0, CHIPS - 1)], ag_send.at[k])
    wait_bytes(SGR.at[pl.ds(0, 3)], sp_send)
    wait_bytes(sg_all.at[pl.ds(0, CHIPS - 1)], sg_send)
    wait_bytes(sg_all, sgx_send)


def hand_over(*refs):
    count = (len(refs) - 2) // 3
    held, in_sem, out_sem = refs[2 * count:3 * count], refs[-2], refs[-1]
    pieces = [(0, pl.ds(n * (OWN // 4), OWN // 4)) for n in range(4)]
    pieces += [(n, pl.ds(0, held[n].shape[0])) for n in range(1, count)]
    into = [
        pltpu.make_async_copy(refs[n].at[rows], held[n].at[rows], in_sem.at[k])
        for k, (n, rows) in enumerate(pieces)
    ]
    out = [
        pltpu.make_async_copy(held[n].at[rows], refs[count + n].at[rows], out_sem.at[k])
        for k, (n, rows) in enumerate(pieces)
    ]
    for copy in into:
        copy.start()
    for k, copy in enumerate(out):
        into[k].wait()
        copy.start()
    for copy in out:
        copy.wait()


def body(tokens, cotangent, gate_taps, key_taps, value_taps, inner_mix, outer_mix, spectrum):
    shape = tokens.shape
    channels = shape[2]
    anywhere = pl.BlockSpec(memory_space=pl.ANY)
    vmem = pl.BlockSpec(memory_space=pltpu.VMEM)
    dma = pltpu.SemaphoreType.DMA
    taps_shape = jax.ShapeDtypeStruct((3, channels), F32)
    matrix = jax.ShapeDtypeStruct((LEN, LEN), F32)
    scratch = [
        pltpu.VMEM((CHUNKS, HALO + ROWS, LANES), BF16),
        pltpu.VMEM((CHUNKS, ROWS, LANES), BF16),
        pltpu.VMEM((CHIPS, LEN, 2 * LANES), BF16),
        pltpu.VMEM((UNITS, 4, SUB, 16, 2 * LANES), BF16),
        pltpu.VMEM((UNITS, SUB, 3 * PART, 2 * LANES), BF16),
        pltpu.VMEM((UNITS, SUB, PART, 2 * LANES), BF16),
        pltpu.VMEM((CHUNKS, CHIPS, 16, 16, 2 * LANES), BF16),
        pltpu.VMEM((CHUNKS, ROWS, LANES), BF16),
        pltpu.VMEM((5, LEN, LEN), BF16),
        pltpu.VMEM((2, 4, PART, 3 * PART), BF16),
        pltpu.VMEM((16, LANES), F32),
        pltpu.VMEM((CHUNKS, 16, LANES), F32),
        pltpu.VMEM((CHUNKS, 16, LANES), F32),
        pltpu.VMEM((CHUNKS, HALO, LANES), F32),
        pltpu.VMEM((CHUNKS, 9, 8, LANES), F32),
        pltpu.VMEM((LEN, LEN), F32),
        pltpu.VMEM((LEN, LEN), F32),
        pltpu.VMEM((2, 2 * PART, LEN), F32),
        pltpu.VMEM((4, CHUNKS, 16, LANES), F32),
        pltpu.VMEM((4, CHUNKS, 16, LANES), F32),
        pltpu.VMEM((CHUNKS, 16, LANES), F32),
        pltpu.VMEM((2, CHIPS, 24, LEN), F32),
        pltpu.VMEM((2, CHIPS, 24, LEN), F32),
        pltpu.VMEM((2, 24, LEN), F32),
        pltpu.VMEM((2, 24, LEN), F32),
        pltpu.VMEM((2, 24, LEN), F32),
        pltpu.VMEM((2, CHIPS, 24, LEN), F32),
        pltpu.VMEM((CHIPS, CHUNKS, 16, LANES), F32),
        pltpu.VMEM((CHIPS, CHUNKS, 16, LANES), F32),
        dma((CHUNKS, 2)), dma((CHUNKS, 2)),
        dma((CHUNKS,)), dma((CHUNKS,)),
        dma((UNITS,)), dma((UNITS,)),
        dma((UNITS, 4)), dma((UNITS,)),
        dma((CHUNKS,)), dma((CHUNKS,)),
        dma((CHUNKS,)), dma((CHUNKS,)),
        dma((CHUNKS,)), dma((CHUNKS,)), dma((CHUNKS,)),
        dma((2,)), dma((2,)),
        dma((2,)), dma((2,)),
        dma((2,)), dma((2,)),
        dma, dma,
        dma, dma,
        dma, dma,
    ]
    outs = pl.pallas_call(
        kernel,
        out_shape=(
            jax.ShapeDtypeStruct((OWN, channels), BF16),
            taps_shape, taps_shape, taps_shape, matrix, matrix,
            jax.ShapeDtypeStruct((LEN, channels), F32),
        ),
        in_specs=[anywhere] * 2 + [vmem] * 6,
        out_specs=(anywhere,) + (vmem,) * 6,
        scratch_shapes=scratch,
        compiler_params=pltpu.CompilerParams(
            collective_id=0, has_side_effects=True, vmem_limit_bytes=62 * 1024 * 1024
        ),
        cost_estimate=pl.CostEstimate(flops=8 * 10**9, bytes_accessed=12 * 10**6, transcendentals=0),
        name="monarch",
    )(
        tokens.reshape(OWN, channels), cotangent.reshape(OWN, channels),
        gate_taps, key_taps, value_taps, inner_mix, outer_mix, spectrum,
    )
    outs = pl.pallas_call(
        hand_over,
        out_shape=tuple(jax.ShapeDtypeStruct(out.shape, out.dtype) for out in outs),
        in_specs=[anywhere] * len(outs),
        out_specs=(anywhere,) * len(outs),
        scratch_shapes=[pltpu.VMEM(out.shape, out.dtype) for out in outs] + [dma((10,)), dma((10,))],
        name="results",
    )(*outs)
    return (outs[0].reshape(shape),) + tuple(outs[1:])


def solution(mesh):
    in_specs = (
        P(("batch", "seq"), None, None),
        P(("batch", "seq"), None, None),
        P(),
        P(),
        P(),
        P(),
        P(),
        P(),
    )
    out_specs = (
        P(("batch", "seq"), None, None),
        P("batch", None),
        P("batch", None),
        P("batch", None),
        P("batch", None),
        P("batch", None),
        P("batch", None),
    )
    return jax.shard_map(body, mesh=mesh, in_specs=in_specs, out_specs=out_specs, check_vma=False)
```

```python
import jax
import jax.numpy as jnp
from jax import lax
from jax.experimental import pallas as pl
from jax.experimental.pallas import tpu as pltpu
from jax.sharding import PartitionSpec as P

MESH = pl.DeviceIdType.MESH
F32 = jnp.float32
BF16 = jnp.bfloat16

LEN = 256
CHIPS = 16
LANES = 128
CHUNKS = 3
HALF = LANES * CHUNKS
ROWS = CHIPS * LEN
OWN = ROWS // 2
HALO = 16
SUB = 8
SPLIT = 16 // SUB
PER_CHUNK = 4 * SPLIT
UNITS = PER_CHUNK * CHUNKS
AHEAD = 1
TURNS = UNITS // 3
LAGS = (0, 1, 2, 3)
PART = 64
OWN_AT, ONE, TWO, PASS = 0, 1, 2, 3

Y, G = 0, 1
ROUTES = (
    (
        (Y, 1, 0, 1, OWN_AT, ONE, 2), (Y, 1, 1, 2, OWN_AT, ONE, 3), (Y, 2, 1, 2, ONE, TWO, 3), (Y, 3, 2, 3, PASS, ONE, 4),
        (G, 1, 3, 2, OWN_AT, ONE, 2), (G, 1, 2, 1, OWN_AT, ONE, 3), (G, 2, 2, 1, ONE, TWO, 3), (G, 3, 1, 0, PASS, ONE, 4),
    ),
    (
        (Y, 1, 0, 3, OWN_AT, TWO, 2), (Y, 1, 0, 1, OWN_AT, ONE, 4), (Y, 1, 1, 2, OWN_AT, ONE, 3), (Y, 2, 3, 2, TWO, TWO, 3),
        (Y, 3, 2, 3, PASS, ONE, 4),
        (G, 1, 3, 0, OWN_AT, TWO, 2), (G, 1, 3, 2, OWN_AT, ONE, 4), (G, 1, 2, 1, OWN_AT, ONE, 3), (G, 2, 0, 1, TWO, TWO, 3),
        (G, 3, 1, 0, PASS, ONE, 4),
    ),
    (
        (Y, 1, 0, 3, OWN_AT, ONE, 3), (Y, 1, 0, 1, OWN_AT, ONE, 4), (Y, 1, 1, 2, OWN_AT, ONE, 3),
        (Y, 3, 3, 2, PASS, TWO, 4), (Y, 3, 2, 3, PASS, TWO, 4),
        (G, 1, 3, 2, OWN_AT, ONE, 3), (G, 1, 2, 3, OWN_AT, ONE, 3), (G, 1, 1, 0, OWN_AT, ONE, 4),
        (G, 3, 2, 1, PASS, ONE, 4), (G, 3, 3, 0, PASS, TWO, 4),
    ),
)
ROUTE_KIND = (0, 0, 1)
NONE, SUM = -1, -2
OWN_Y = (
    ((0, 1, 2, 3), (0, 1, 2, 3), (NONE, 0, 1, SUM), (NONE, NONE, 0, NONE)),
    ((0, 1, 2, 3), (0, 1, 2, 3), (NONE, 0, 1, 0), (NONE, NONE, SUM, SUM)),
)
PASS_Y = (
    ((0, 0, 3, 0), (NONE, NONE, 2, NONE), (NONE, NONE, 1, NONE), (NONE, NONE, 0, NONE)),
    ((0, 0, 3, 2), (NONE, NONE, 2, NONE), (NONE, NONE, 1, 0), (NONE, NONE, NONE, NONE)),
)
OWN_G = (
    ((0, 1, 2, 3), (0, 1, 2, 3), (SUM, 2, 3, NONE), (NONE, 3, NONE, NONE)),
    ((0, 1, 2, 3), (0, 1, 2, 3), (1, SUM, 3, NONE), (SUM, NONE, NONE, NONE)),
)
PASS_G = (
    ((0, 0, 0, 0), (NONE, 1, NONE, NONE), (NONE, 2, NONE, NONE), (NONE, 3, NONE, NONE)),
    ((0, 0, 1, 0), (NONE, NONE, 2, 3), (NONE, NONE, 3, 2), (NONE, NONE, NONE, NONE)),
)
OUTER_ROWS = (((0, 1, 2, 3), (NONE, NONE, 3, NONE)), ((0, 1, 2, 3), (NONE, NONE, 3, 2)))
OUTER_COLS = (
    (
        ((0, 1, 2, 3), (NONE, 0, 1, NONE), (NONE, NONE, 0, NONE)),
        ((NONE, NONE, 2, NONE), (NONE, NONE, 1, NONE), (NONE, NONE, 0, NONE)),
    ),
    (
        ((0, 1, 2, 3), (NONE, 0, 1, 0), (NONE, NONE, NONE, NONE)),
        ((NONE, NONE, 2, NONE), (NONE, NONE, 1, 0), (NONE, NONE, NONE, NONE)),
    ),
)


def dot(a, b):
    return jnp.dot(a, b, preferred_element_type=F32)


def dot_lanes(a, b):
    return lax.dot_general(a, b, (((1,), (1,)), ((), ())), preferred_element_type=F32)


def strict_lower(value, first_row):
    rows = lax.broadcasted_iota(jnp.int32, value.shape, 0) + first_row
    cols = lax.broadcasted_iota(jnp.int32, value.shape, 1)
    return jnp.where(rows > cols, value, 0.0)


def kernel(
    tok, cot, gate_taps, key_taps, value_taps, inner_mix, outer_mix, spectrum,
    out_tok, out_gate, out_key, out_value, out_inner, out_outer, out_spec,
    T, CT, AB, S, W, PS, F, GT, MAT, MIX, CARRY, HB, HR, LB, TA,
    inner_acc, outer_acc, outer_parts, SGP, SGR, SG, red_send, red_recv, red_sum, red_sib, total, gathered,
    sg_all, sg_sib,
    in_sem, in_send, halo_sem, halo_send, x_sem, x_send, z_sem, z_send, f_sem, r_send, hb_sem, hb_send,
    out_local, out_send, out_recv, sib_sem, sib_send, rs_sem, rs_send, ag_sem, ag_send,
    sp_sem, sp_send, sg_sem, sg_send, sgx_sem, sgx_send,
):
    batch = lax.axis_index("batch")
    seq = lax.axis_index("seq")
    core = seq % 2
    chip = seq // 2
    cz = chip // 4
    cx = chip % 4
    other = 1 - core
    sibling = (batch, chip * 2 + other)

    def chip_dev(q):
        return (batch, q * 2 + core)

    def peer(d):
        return ((cz + d // 4) % 4) * 4 + (cx + d % 4) % 4

    def on_plane(x):
        return chip_dev(cz * 4 + x)

    def at_plane(values):
        out = jnp.int32(values[3])
        for plane in range(3):
            out = jnp.where(cz == plane, jnp.int32(values[plane]), out)
        return out

    def clear(u, carry):
        def rows(j, c):
            W[u, j, PART:] = jnp.zeros((2 * PART, 2 * LANES), BF16)
            return c

        return lax.fori_loop(0, SUB, rows, carry)

    lax.fori_loop(0, UNITS, clear, 0)
    barrier = pltpu.get_barrier_semaphore()

    def greet(d, carry):
        pl.semaphore_signal(barrier, inc=1, device_id=chip_dev(peer(d)), device_id_type=MESH)
        return carry

    lax.fori_loop(1, CHIPS, greet, 0)
    pl.semaphore_signal(barrier, inc=1, device_id=sibling, device_id_type=MESH)
    pl.semaphore_wait(barrier, CHIPS)

    def remote(src, dst, send, recv, device):
        return pltpu.make_async_remote_copy(
            src_ref=src, dst_ref=dst, send_sem=send, recv_sem=recv,
            device_id=device, device_id_type=MESH,
        )

    def wait_bytes(ref, sem):
        pltpu.make_async_copy(ref, ref, sem).wait()

    my_rows = pl.ds(pl.multiple_of(core * OWN, OWN), OWN)
    halo_rows = pl.ds(pl.multiple_of(HALO + core * OWN, HALO), OWN)

    def lanes_of(c, ch):
        return pl.ds(pl.multiple_of(c * HALF + ch * LANES, LANES), LANES)

    def start_inputs(ch, carry):
        remote(tok.at[:, lanes_of(other, ch)], T.at[ch, halo_rows], in_send.at[ch, 0], in_sem.at[ch, 0], sibling).start()
        remote(cot.at[:, lanes_of(other, ch)], CT.at[ch, my_rows], in_send.at[ch, 1], in_sem.at[ch, 1], sibling).start()
        pltpu.make_async_copy(tok.at[:, lanes_of(core, ch)], T.at[ch, halo_rows], in_sem.at[ch, 0]).start()
        pltpu.make_async_copy(cot.at[:, lanes_of(core, ch)], CT.at[ch, my_rows], in_sem.at[ch, 1]).start()
        return carry

    lax.fori_loop(0, CHUNKS, start_inputs, 0)

    row_id = lax.broadcasted_iota(jnp.int32, (LEN, LEN), 0)
    col_id = lax.broadcasted_iota(jnp.int32, (LEN, LEN), 1)
    for at, weights in ((0, inner_mix), (2, outer_mix)):
        full = jnp.where(
            row_id > col_id, weights[...].astype(F32), jnp.where(row_id == col_id, 1.0, 0.0)
        )
        MAT[at] = full.astype(BF16)
        MAT[at + 1] = jnp.transpose(full).astype(BF16)
    MAT[4] = jnp.where(col_id == (row_id % 16) * 16 + row_id // 16, 1.0, 0.0).astype(BF16)
    slot_row = lax.broadcasted_iota(jnp.int32, (LEN, 3 * PART), 0)
    slot_col = lax.broadcasted_iota(jnp.int32, (LEN, 3 * PART), 1)
    eye_row = lax.broadcasted_iota(jnp.int32, (PART, 3 * PART), 0)
    eye_col = lax.broadcasted_iota(jnp.int32, (PART, 3 * PART), 1)
    for kind in range(2):
        for n, (table, mat) in enumerate(((OWN_Y, 2), (PASS_Y, 2), (OWN_G, 3), (PASS_G, 3))):
            to, *slots = table[kind]
            pick = jnp.zeros((LEN, 3 * PART), F32)
            add = jnp.zeros((PART, 3 * PART), F32)
            for k, planes in enumerate(slots):
                plane = at_plane(planes)
                here = jnp.logical_and(slot_col // PART == k, slot_row == plane * PART + slot_col % PART)
                pick = jnp.where(here, 1.0, pick)
                same = jnp.logical_and(eye_col == eye_row + k * PART, plane == SUM)
                add = jnp.where(same, 1.0, add)
            rows = MAT[mat, pl.ds(pl.multiple_of(at_plane(to) * PART, PART), PART)]
            MIX[kind, n] = (dot(rows, pick.astype(BF16)) + add).astype(BF16)
    inner_acc[...] = jnp.zeros_like(inner_acc)
    outer_acc[...] = jnp.zeros_like(outer_acc)
    outer_parts[...] = jnp.zeros_like(outer_parts)
    TA[...] = jnp.zeros_like(TA)

    def send_halo(ch, carry):
        wait_bytes(T.at[ch, pl.ds(HALO, ROWS)], in_sem.at[ch, 0])

        @pl.when(chip < CHIPS - 1)
        def _():
            remote(
                T.at[ch, pl.ds(ROWS, HALO)], T.at[ch, pl.ds(0, HALO)],
                halo_send.at[ch], halo_sem.at[ch], chip_dev(chip + 1),
            ).start()

        @pl.when(chip == 0)
        def _():
            T[ch, 0:HALO] = jnp.zeros((HALO, LANES), BF16)

        wait_bytes(CT.at[ch], in_sem.at[ch, 1])
        return carry

    def taps_of(ref, ch):
        block = ref[:, lanes_of(core, ch)]
        return block[0:1], block[1:2], block[2:3]

    def shifted_rows(ch, i):
        ext = T[ch, pl.ds(pl.multiple_of(i * LEN, LEN), LEN + HALO)].astype(F32)
        return ext[HALO:], pltpu.roll(ext, 1, 0)[HALO:], pltpu.roll(ext, 2, 0)[HALO:]

    def conv(taps, x):
        return taps[0] * x[0] + taps[1] * x[1] + taps[2] * x[2]

    def block_rows(i):
        return pl.ds(pl.multiple_of(i * LEN, LEN), LEN)

    def before(ch, carry):
        gt, kt, vt = taps_of(gate_taps, ch), taps_of(key_taps, ch), taps_of(value_taps, ch)
        send_halo(ch, 0)

        def pair(step, c):
            p = CHIPS // 2 - 1 - step

            @pl.when(jnp.logical_and(p == 0, chip > 0))
            def _():
                wait_bytes(T.at[ch, pl.ds(0, HALO)], halo_sem.at[ch])

            products = []
            for b in range(2):
                i = 2 * p + b
                x = shifted_rows(ch, i)
                product = (conv(kt, x) * conv(vt, x)).astype(BF16)
                products.append(product)
                grad_mixed = CT[ch, block_rows(i)].astype(F32) * conv(gt, x)
                AB[i, :, LANES:] = grad_mixed.astype(BF16)
            pre = dot(MAT[0], jnp.concatenate(products, 1))
            scale = spectrum[:, lanes_of(core, ch)]
            for b in range(2):
                AB[2 * p + b, :, :LANES] = (pre[:, b * LANES:(b + 1) * LANES] * scale).astype(BF16)
            return c

        lax.fori_loop(0, CHIPS // 2, pair, 0)

        def quarter(t, c):
            u0 = ch * PER_CHUNK + t * SPLIT

            def regroup(x, c):
                j = 4 * x + t
                rows = AB[:, pl.ds(pl.multiple_of(j * 16, 16), 16)].reshape(LEN, 2 * LANES)
                made = dot(MAT[4], rows).astype(BF16).reshape(16, 16, 2 * LANES)
                for h in range(SPLIT):
                    S[u0 + h, x] = made[h * SUB:(h + 1) * SUB]
                return c

            lax.fori_loop(0, 4, regroup, 0)

            return c

        lax.fori_loop(0, 4, quarter, 0)
        return carry

    def slot(ref, u, k, array):
        return ref.at[u, :, k * PART:(k + 1) * PART, array * LANES:(array + 1) * LANES]

    def sends(u, route, step):
        for array, when, source, target, here, there, _ in ROUTES[route]:
            if when == step:
                @pl.when(cz == source)
                def _(array=array, target=target, here=here, there=there):
                    origin = slot(PS, u, 0, array) if here == PASS else slot(W, u, here, array)
                    remote(
                        origin, slot(W, u, there, array), z_send.at[u],
                        z_sem.at[u, 2 * array + there - 1], chip_dev(target * 4 + cx),
                    ).start()

    def receives(u, route, step):
        for array, _, _, target, _, there, when in ROUTES[route]:
            if when == step:
                @pl.when(cz == target)
                def _(array=array, there=there):
                    wait_bytes(slot(W, u, there, array), z_sem.at[u, 2 * array + there - 1])

    def pair_of(u, j, array, rows=3 * PART):
        lanes = slice(array * LANES, (array + 1) * LANES)
        return jnp.concatenate([W[u, j, 0:rows, lanes], W[u, j + 1, 0:rows, lanes]], 1)

    def hand_out(u):
        mine = pl.ds(pl.multiple_of(cx * 16, 16), 16)

        def send(d, c):
            x = (cx + d) % 4
            remote(S.at[u, x], W.at[u, :, mine], x_send.at[u], x_sem.at[u], on_plane(x)).start()
            return c

        lax.fori_loop(1, 4, send, 0)
        pltpu.make_async_copy(S.at[u, cx], W.at[u, :, mine], x_sem.at[u]).start()

    def step1(u, route):
        wait_bytes(W.at[u, :, 0:PART], x_sem.at[u])
        sends(u, route, 1)

    def step2(u, route):
        receives(u, route, 2)
        sends(u, route, 2)

    def step3(u, route):
        receives(u, route, 3)
        kind = ROUTE_KIND[route]
        for array in (Y, G):
            single = 2 if array == Y else 1
            used = (3 if kind == 0 else 2) * PART
            passes = cz == single if kind == 0 else cz >= 2

            @pl.when(passes)
            def _(array=array):
                def pair(p, c):
                    j = 2 * p
                    mix = MIX[kind, 2 * array + 1, :, 0:used]
                    total = dot(mix, pair_of(u, j, array, used)).astype(BF16)
                    for b in range(2):
                        PS[u, j + b, :, array * LANES:(array + 1) * LANES] = total[:, b * LANES:(b + 1) * LANES]
                    return c

                lax.fori_loop(0, SUB // 2, pair, 0)
        sends(u, route, 3)

    def step4(u, route):
        receives(u, route, 4)
        kind = ROUTE_KIND[route]
        ch, t, h = u // PER_CHUNK, (u % PER_CHUNK) // SPLIT, u % SPLIT
        back = F.at[ch, 4 * cx + t, pl.ds(h * SUB, SUB)]

        def pair(p, c):
            j = 2 * p
            inner, grads = pair_of(u, j, Y), pair_of(u, j, G)
            mixed = dot(MIX[kind, 0], inner).astype(BF16)
            grad_inner = dot(MIX[kind, 2], grads).astype(BF16)
            outer_parts[kind, :, 0:3 * PART] += dot_lanes(grads[0:2 * PART], inner)
            terms = jnp.sum(
                grad_inner.astype(F32) * inner[0:PART].astype(F32), axis=0, keepdims=True
            )
            for b in range(2):
                at = slice(b * LANES, (b + 1) * LANES)
                S[u, :, j + b, :, :LANES] = mixed[:, at].reshape(4, 16, LANES)
                S[u, :, j + b, :, LANES:] = grad_inner[:, at].reshape(4, 16, LANES)
                SGP[t, ch, pl.ds(h * SUB + j + b, 1)] = terms[:, at]
            return c

        wait_bytes(S.at[u, pl.ds(0, 3)], x_send.at[u])
        lax.fori_loop(0, SUB // 2, pair, 0)

        def send(d, c):
            x = (cx + d) % 4
            remote(
                S.at[u, x], back,
                r_send.at[ch], f_sem.at[ch], on_plane(x),
            ).start()
            return c

        lax.fori_loop(1, 4, send, 0)
        pltpu.make_async_copy(
            S.at[u, cx], back, f_sem.at[ch]
        ).start()

    def place_outer():
        cols = lax.broadcasted_iota(jnp.int32, (PART, LEN), 1)
        for kind in range(2):
            for k in range(2):
                row = at_plane(OUTER_ROWS[kind][k])
                part = outer_parts[kind, k * PART:(k + 1) * PART]
                total = jnp.zeros((PART, LEN), F32)
                for n, planes in enumerate(OUTER_COLS[kind][k]):
                    plane = at_plane(planes)
                    moved = pltpu.roll(part, (plane * PART + LEN - n * PART) % LEN, 1)
                    total = jnp.where(cols // PART == plane, moved, total)

                @pl.when(row != NONE)
                def _(row=row, total=total):
                    outer_acc[pl.ds(pl.multiple_of(row * PART, PART), PART)] += total

    def scatter_start(k, acc, extra):
        red_send[k, :, 0:16] = acc[...].reshape(CHIPS, 16, LEN)
        red_send[k, :, 16:24] = jnp.zeros((CHIPS, 8, LEN), F32)
        extra()

        def send(d, c):
            q = peer(d)
            remote(red_send.at[k, q], red_recv.at[k, chip], rs_send.at[k], rs_sem.at[k], chip_dev(q)).start()
            return c

        lax.fori_loop(1, CHIPS, send, 0)
        pltpu.make_async_copy(red_send.at[k, chip], red_recv.at[k, chip], rs_sem.at[k]).start()

    def swap_start(k):
        wait_bytes(red_recv.at[k], rs_sem.at[k])
        red_sum[k] = jnp.sum(red_recv[k], axis=0)
        remote(red_sum.at[k], red_sib.at[k], sib_send.at[k], sib_sem.at[k], sibling).start()

    def gather_start(k):
        wait_bytes(red_sib.at[k], sib_sem.at[k])
        total[k, 0:16] = red_sum[k, 0:16] + red_sib[k, 0:16]
        total[k, 16:24] = jnp.zeros((8, LEN), F32)
        total[k, pl.ds(16 + core, 1)] = red_sum[k, 16:17]
        total[k, pl.ds(16 + other, 1)] = red_sib[k, 16:17]

        def send(d, c):
            remote(total.at[k], gathered.at[k, chip], ag_send.at[k], ag_sem.at[k], chip_dev(peer(d))).start()
            return c

        lax.fori_loop(1, CHIPS, send, 0)
        pltpu.make_async_copy(total.at[k], gathered.at[k, chip], ag_sem.at[k]).start()

    def write_matrix(k, out):
        wait_bytes(gathered.at[k], ag_sem.at[k])
        out[...] = strict_lower(gathered[k, :, 0:16].reshape(LEN, LEN), 0)

    def spectrum_scatter():
        def send(d, c):
            t = (cz + d) % 4
            remote(SGP.at[t], SGR.at[cz], sp_send, sp_sem, chip_dev(t * 4 + cx)).start()
            return c

        lax.fori_loop(1, 4, send, 0)
        pltpu.make_async_copy(SGP.at[cz], SGR.at[cz], sp_sem).start()

    def spectrum_start():
        wait_bytes(SGR, sp_sem)
        here = pl.ds(pl.multiple_of((4 * cx + cz) * 16, 16), 16)
        for ch in range(CHUNKS):
            SG[ch] = jnp.sum(SGR[:, ch], axis=0) / spectrum[here, lanes_of(core, ch)]

        def send(d, c):
            remote(SG, sg_all.at[chip], sg_send, sg_sem, chip_dev(peer(d))).start()
            return c

        lax.fori_loop(1, CHIPS, send, 0)
        pltpu.make_async_copy(SG, sg_all.at[chip], sg_sem).start()

    def spectrum_swap():
        wait_bytes(sg_all, sg_sem)
        remote(sg_all, sg_sib, sgx_send, sgx_sem, sibling).start()

    def spectrum_write():
        wait_bytes(sg_sib, sgx_sem)

        def rows(q, c):
            at = pl.ds(pl.multiple_of((4 * (q % 4) + q // 4) * 16, 16), 16)
            for ch in range(CHUNKS):
                out_spec[at, lanes_of(core, ch)] = sg_all[q, ch]
                out_spec[at, lanes_of(other, ch)] = sg_sib[q, ch]
            return c

        lax.fori_loop(0, CHIPS, rows, 0)

    def after(ch):
        gt, kt, vt = taps_of(gate_taps, ch), taps_of(key_taps, ch), taps_of(value_taps, ch)
        scale = spectrum[:, lanes_of(core, ch)]
        wait_bytes(F.at[ch], f_sem.at[ch])

        def regroup(j, c):
            rows = F[ch, j].reshape(LEN, 2 * LANES)
            AB[:, pl.ds(pl.multiple_of(j * 16, 16), 16)] = dot(MAT[4], rows).astype(BF16).reshape(
                16, 16, 2 * LANES
            )
            return c

        lax.fori_loop(0, CHIPS, regroup, 0)
        CARRY[...] = jnp.zeros_like(CARRY)

        def pair(step, c):
            p = CHIPS // 2 - 1 - step
            scaled = jnp.concatenate(
                [(AB[2 * p + b, :, LANES:].astype(F32) * scale).astype(BF16) for b in range(2)], 1
            )
            shifts = [shifted_rows(ch, 2 * p + b) for b in range(2)]
            keys = [conv(kt, x) for x in shifts]
            values = [conv(vt, x) for x in shifts]
            product = jnp.concatenate([(keys[b] * values[b]).astype(BF16) for b in range(2)], 1)
            inner_acc[...] += dot_lanes(scaled, product)
            grad_product = dot(MAT[1], scaled)
            for b in (1, 0):
                i = 2 * p + b
                x = shifts[b]
                gp = grad_product[:, b * LANES:(b + 1) * LANES]
                grads = (
                    CT[ch, block_rows(i)].astype(F32) * AB[i, :, :LANES].astype(F32),
                    gp * values[b],
                    gp * keys[b],
                )
                for k in range(3):
                    for s in range(3):
                        TA[ch, 3 * k + s] += jnp.sum(
                            (grads[k] * x[s]).reshape(LEN // 8, 8, LANES), axis=0
                        )
                u = [gt[s] * grads[0] + kt[s] * grads[1] + vt[s] * grads[2] for s in range(3)]
                ext1 = jnp.concatenate([u[1], CARRY[0:8]], 0)
                ext2 = jnp.concatenate([u[2], CARRY[8:16]], 0)
                total = u[0] + pltpu.roll(ext1, LEN + 7, 0)[:LEN] + pltpu.roll(ext2, LEN + 6, 0)[:LEN]
                GT[ch, block_rows(i)] = total.astype(BF16)
                CARRY[0:8] = u[1][0:8]
                CARRY[8:16] = u[2][0:8]
                if b == 1:
                    @pl.when(p == CHIPS // 2 - 1)
                    def _():
                        LB[ch] = total[LEN - HALO:]
            return c

        lax.fori_loop(0, CHIPS // 2, pair, 0)
        HB[ch] = CARRY[...]

        @pl.when(chip > 0)
        def _():
            remote(HB.at[ch], HR.at[ch], hb_send.at[ch], hb_sem.at[ch], chip_dev(chip - 1)).start()

    def finish(ch):
        @pl.when(chip < CHIPS - 1)
        def _():
            wait_bytes(HR.at[ch], hb_sem.at[ch])
            row = lax.broadcasted_iota(jnp.int32, (HALO, LANES), 0)
            one, two = HR[ch, 0:8], HR[ch, 8:16]
            last = jnp.where(row == HALO - 1, one[0:1] + two[1:2], jnp.where(row == HALO - 2, two[0:1], 0.0))
            GT[ch, ROWS - HALO:ROWS] = (LB[ch] + last).astype(BF16)

        pltpu.make_async_copy(GT.at[ch, my_rows], out_tok.at[:, lanes_of(core, ch)], out_local.at[ch]).start()
        theirs = pl.ds(pl.multiple_of(other * OWN, OWN), OWN)
        remote(
            GT.at[ch, theirs], out_tok.at[:, lanes_of(core, ch)], out_send.at[ch], out_recv.at[ch], sibling
        ).start()

    before(0, 0)

    steps = (step1, step2, step3, step4)

    def step(n, k):
        at = k - LAGS[n - 1]

        @pl.when(jnp.logical_and(at >= 0, at < TURNS))
        def _():
            for route in range(len(ROUTES)):
                steps[n - 1](len(ROUTES) * at + route, route)

    def hand_out_turn(at):
        for route in range(len(ROUTES)):
            hand_out(len(ROUTES) * at + route)

    def turn(k, carry):
        @pl.when(k + AHEAD < TURNS)
        def _():
            hand_out_turn(k + AHEAD)

        step(2, k)
        step(3, k)
        step(4, k)
        step(1, k)
        return carry

    for at in range(AHEAD):
        hand_out_turn(at)
    first = -(-PER_CHUNK // len(ROUTES)) + LAGS[3] + 2
    second = -(-2 * PER_CHUNK // len(ROUTES)) + LAGS[3] + 1
    lax.fori_loop(0, 0, turn, 0)
    before(1, 0)
    lax.fori_loop(0, 2, turn, 0)
    before(2, 0)
    lax.fori_loop(2, first, turn, 0)
    after(0)
    lax.fori_loop(first, second, turn, 0)
    after(1)
    finish(0)
    lax.fori_loop(second, TURNS + LAGS[3], turn, 0)
    place_outer()
    scatter_start(0, outer_acc, lambda: None)
    spectrum_scatter()
    after(2)

    def put_taps():
        for n in range(9 * CHUNKS):
            k, ch = n // CHUNKS, n % CHUNKS
            at = slice((n % 2) * LANES, (n % 2 + 1) * LANES)
            red_send[1, n // 2, 16:17, at] = jnp.sum(TA[ch, k], axis=0, keepdims=True)

    scatter_start(1, inner_acc, put_taps)
    swap_start(0)
    spectrum_start()
    finish(1)
    gather_start(0)
    swap_start(1)
    finish(2)
    spectrum_swap()
    gather_start(1)
    write_matrix(0, out_outer)
    spectrum_write()
    write_matrix(1, out_inner)
    for n in range(9 * CHUNKS):
        k, ch = n // CHUNKS, n % CHUNKS
        out = (out_gate, out_key, out_value)[k // 3]
        at = slice((n % 2) * LANES, (n % 2 + 1) * LANES)
        for c in range(2):
            lanes = slice(c * HALF + ch * LANES, c * HALF + (ch + 1) * LANES)
            out[k % 3:k % 3 + 1, lanes] = gathered[1, n // 2, 16 + c:17 + c, at]

    for ch in range(CHUNKS):
        wait_bytes(T.at[ch, pl.ds(0, OWN)], in_send.at[ch, 0])
        wait_bytes(CT.at[ch, pl.ds(0, OWN)], in_send.at[ch, 1])

        @pl.when(chip < CHIPS - 1)
        def _():
            wait_bytes(T.at[ch, pl.ds(0, HALO)], halo_send.at[ch])

        @pl.when(chip > 0)
        def _():
            wait_bytes(HB.at[ch], hb_send.at[ch])

        wait_bytes(F.at[ch, pl.ds(0, 12)], r_send.at[ch])
        wait_bytes(GT.at[ch, pl.ds(0, OWN)], out_local.at[ch])
        wait_bytes(GT.at[ch, pl.ds(0, OWN)], out_send.at[ch])
        wait_bytes(GT.at[ch, pl.ds(0, OWN)], out_recv.at[ch])
    def sent(at, carry):
        for route, lines in enumerate(ROUTES):
            u = len(ROUTES) * at + route
            for source in range(4):
                count = sum(line[2] == source for line in lines)

                @pl.when(cz == source)
                def _(count=count, u=u):
                    wait_bytes(W.at[u, :, 0:count * PART, 0:LANES], z_send.at[u])

        return carry

    lax.fori_loop(0, TURNS, sent, 0)
    for k in range(2):
        wait_bytes(red_sum.at[k], sib_send.at[k])
        wait_bytes(red_send.at[k, pl.ds(0, CHIPS - 1)], rs_send.at[k])
        wait_bytes(gathered.at[k, pl.ds(0, CHIPS - 1)], ag_send.at[k])
    wait_bytes(SGR.at[pl.ds(0, 3)], sp_send)
    wait_bytes(sg_all.at[pl.ds(0, CHIPS - 1)], sg_send)
    wait_bytes(sg_all, sgx_send)


def hand_over(*refs):
    count = (len(refs) - 2) // 3
    held, in_sem, out_sem = refs[2 * count:3 * count], refs[-2], refs[-1]
    pieces = [(0, pl.ds(n * (OWN // 4), OWN // 4)) for n in range(4)]
    pieces += [(n, pl.ds(0, held[n].shape[0])) for n in range(1, count)]
    into = [
        pltpu.make_async_copy(refs[n].at[rows], held[n].at[rows], in_sem.at[k])
        for k, (n, rows) in enumerate(pieces)
    ]
    out = [
        pltpu.make_async_copy(held[n].at[rows], refs[count + n].at[rows], out_sem.at[k])
        for k, (n, rows) in enumerate(pieces)
    ]
    for copy in into:
        copy.start()
    for k, copy in enumerate(out):
        into[k].wait()
        copy.start()
    for copy in out:
        copy.wait()


def body(tokens, cotangent, gate_taps, key_taps, value_taps, inner_mix, outer_mix, spectrum):
    shape = tokens.shape
    channels = shape[2]
    anywhere = pl.BlockSpec(memory_space=pl.ANY)
    vmem = pl.BlockSpec(memory_space=pltpu.VMEM)
    dma = pltpu.SemaphoreType.DMA
    taps_shape = jax.ShapeDtypeStruct((3, channels), F32)
    matrix = jax.ShapeDtypeStruct((LEN, LEN), F32)
    scratch = [
        pltpu.VMEM((CHUNKS, HALO + ROWS, LANES), BF16),
        pltpu.VMEM((CHUNKS, ROWS, LANES), BF16),
        pltpu.VMEM((CHIPS, LEN, 2 * LANES), BF16),
        pltpu.VMEM((UNITS, 4, SUB, 16, 2 * LANES), BF16),
        pltpu.VMEM((UNITS, SUB, 3 * PART, 2 * LANES), BF16),
        pltpu.VMEM((UNITS, SUB, PART, 2 * LANES), BF16),
        pltpu.VMEM((CHUNKS, CHIPS, 16, 16, 2 * LANES), BF16),
        pltpu.VMEM((CHUNKS, ROWS, LANES), BF16),
        pltpu.VMEM((5, LEN, LEN), BF16),
        pltpu.VMEM((2, 4, PART, 3 * PART), BF16),
        pltpu.VMEM((16, LANES), F32),
        pltpu.VMEM((CHUNKS, 16, LANES), F32),
        pltpu.VMEM((CHUNKS, 16, LANES), F32),
        pltpu.VMEM((CHUNKS, HALO, LANES), F32),
        pltpu.VMEM((CHUNKS, 9, 8, LANES), F32),
        pltpu.VMEM((LEN, LEN), F32),
        pltpu.VMEM((LEN, LEN), F32),
        pltpu.VMEM((2, 2 * PART, LEN), F32),
        pltpu.VMEM((4, CHUNKS, 16, LANES), F32),
        pltpu.VMEM((4, CHUNKS, 16, LANES), F32),
        pltpu.VMEM((CHUNKS, 16, LANES), F32),
        pltpu.VMEM((2, CHIPS, 24, LEN), F32),
        pltpu.VMEM((2, CHIPS, 24, LEN), F32),
        pltpu.VMEM((2, 24, LEN), F32),
        pltpu.VMEM((2, 24, LEN), F32),
        pltpu.VMEM((2, 24, LEN), F32),
        pltpu.VMEM((2, CHIPS, 24, LEN), F32),
        pltpu.VMEM((CHIPS, CHUNKS, 16, LANES), F32),
        pltpu.VMEM((CHIPS, CHUNKS, 16, LANES), F32),
        dma((CHUNKS, 2)), dma((CHUNKS, 2)),
        dma((CHUNKS,)), dma((CHUNKS,)),
        dma((UNITS,)), dma((UNITS,)),
        dma((UNITS, 4)), dma((UNITS,)),
        dma((CHUNKS,)), dma((CHUNKS,)),
        dma((CHUNKS,)), dma((CHUNKS,)),
        dma((CHUNKS,)), dma((CHUNKS,)), dma((CHUNKS,)),
        dma((2,)), dma((2,)),
        dma((2,)), dma((2,)),
        dma((2,)), dma((2,)),
        dma, dma,
        dma, dma,
        dma, dma,
    ]
    outs = pl.pallas_call(
        kernel,
        out_shape=(
            jax.ShapeDtypeStruct((OWN, channels), BF16),
            taps_shape, taps_shape, taps_shape, matrix, matrix,
            jax.ShapeDtypeStruct((LEN, channels), F32),
        ),
        in_specs=[anywhere] * 2 + [vmem] * 6,
        out_specs=(anywhere,) + (vmem,) * 6,
        scratch_shapes=scratch,
        compiler_params=pltpu.CompilerParams(
            collective_id=0, has_side_effects=True, vmem_limit_bytes=62 * 1024 * 1024
        ),
        cost_estimate=pl.CostEstimate(flops=8 * 10**9, bytes_accessed=12 * 10**6, transcendentals=0),
        name="monarch",
    )(
        tokens.reshape(OWN, channels), cotangent.reshape(OWN, channels),
        gate_taps, key_taps, value_taps, inner_mix, outer_mix, spectrum,
    )
    outs = pl.pallas_call(
        hand_over,
        out_shape=tuple(jax.ShapeDtypeStruct(out.shape, out.dtype) for out in outs),
        in_specs=[anywhere] * len(outs),
        out_specs=(anywhere,) * len(outs),
        scratch_shapes=[pltpu.VMEM(out.shape, out.dtype) for out in outs] + [dma((10,)), dma((10,))],
        name="results",
    )(*outs)
    return (outs[0].reshape(shape),) + tuple(outs[1:])


def solution(mesh):
    in_specs = (
        P(("batch", "seq"), None, None),
        P(("batch", "seq"), None, None),
        P(),
        P(),
        P(),
        P(),
        P(),
        P(),
    )
    out_specs = (
        P(("batch", "seq"), None, None),
        P("batch", None),
        P("batch", None),
        P("batch", None),
        P("batch", None),
        P("batch", None),
        P("batch", None),
    )
    return jax.shard_map(body, mesh=mesh, in_specs=in_specs, out_specs=out_specs, check_vma=False)
```
